32 devices in a mesh: seq: 4 (over y, x), chan: 8 (over z, core).
Axes of the slice: x: 2, y: 2, z: 4, core: 2. Of those that a mesh axis runs over, the one named last changes fastest.
Arguments:
- post_gate: bfloat16 [512, 4096], P('chan', 'seq'), may hold values from -6 to 6
- pre_gate: bfloat16 [512, 4096], P('chan', 'seq'), may hold values from -6 to 6
- signal: bfloat16 [512, 4096], P('chan', 'seq'), may hold values from -6 to 6
- cotangent: bfloat16 [512, 4096], P('chan', 'seq'), may hold values from -6 to 6
- filter_taps: float32 [512, 4096], P('chan', 'seq'), may hold values from -0.09375 to 0.09375
- skip_gain: float32 [512], P('chan'), may hold values from -4 to 4
Outputs:
- output: bfloat16 [512, 4096], P('chan', 'seq')
- d_post: bfloat16 [512, 4096], P('chan', 'seq')
- d_pre: bfloat16 [512, 4096], P('chan', 'seq')
- d_signal: bfloat16 [512, 4096], P('chan', 'seq')
- d_skip: float32 [512], P('chan')
- d_filter: float32 [512, 4096], P('chan', 'seq')
The draws below stay inside these ranges and needn't reach their ends.
All inputs are finite; a program needn't handle non-finite values.
Results may differ from the reference program's by a relative error of at most 0.004.
Values sent between devices are 32-bit elements; how exact they have to be, the bound alone decides.
No kernel may reach another device: no remote copies, remote signals or barrier semaphores. Data moves between devices by JAX's collectives and lax.ppermute only.
A program may use at most 64 MiB of HBM per device.

```python
import jax
import jax.numpy as jnp

CHANNELS = 512
TOKENS = 4096


def steps_of(stream_key, dims, split, smallest, high):
    def one(dim, shards_of):
        heights = jax.random.uniform(jax.random.fold_in(jax.random.fold_in(stream_key, 6), dim), (shards_of,), jnp.float32, smallest / len(split), high / len(split))
        return jnp.repeat(jnp.exp(heights), dims[dim] // shards_of).reshape((-1,) + (1,) * (len(dims) - dim - 1))

    gain = one(*split[0])
    for cut in split[1:]:
        gain = gain * one(*cut)
    return gain


def gaussian(rng, shape, width, limit, shards=(), held_as=jnp.bfloat16):
    array = width * jax.random.normal(rng, shape, jnp.float32)
    if shards:
        array = array * steps_of(rng, shape, shards, -0.22, 0.18)
    return jnp.clip(array, -limit, limit).astype(held_as)


def setup_inputs(seed: int = 0) -> dict:
    seeds = jax.random.split(jax.random.key(seed), 7)
    post_gate = gaussian(seeds[0], (CHANNELS, TOKENS), 1.0, 6.0, ((0, 8), (1, 4)))
    pre_gate = gaussian(seeds[1], (CHANNELS, TOKENS), 1.0, 6.0, ((0, 8), (1, 4)))
    signal = gaussian(seeds[2], (CHANNELS, TOKENS), 1.0, 6.0, ((0, 8), (1, 4)))
    cotangent = gaussian(seeds[3], (CHANNELS, TOKENS), 1.0, 6.0, ((0, 8), (1, 4)))
    filter_taps = gaussian(seeds[4], (CHANNELS, TOKENS), TOKENS ** -0.5, 0.09375, ((0, 8), (1, 4)), jnp.float32)
    skip_gain = gaussian(seeds[5], (CHANNELS,), 1.0, 4.0, ((0, 8),), jnp.float32)
    return {"post_gate": post_gate, "pre_gate": pre_gate, "signal": signal, "cotangent": cotangent, "filter_taps": filter_taps, "skip_gain": skip_gain}


def spectra(values):
    return jnp.fft.rfft(values, n=2 * TOKENS, axis=1)


def to_time(spectrum):
    return jnp.fft.irfft(spectrum, n=2 * TOKENS, axis=1)[:, :TOKENS].astype(jnp.float32)


def reference(post_gate, pre_gate, signal, cotangent, filter_taps, skip_gain):
    post_f = post_gate.astype(jnp.float32)
    pre_f = pre_gate.astype(jnp.float32)
    signal_f = signal.astype(jnp.float32)
    gated = pre_f * signal_f
    filter_spec = spectra(filter_taps)
    gated_spec = spectra(gated)
    conv_part = to_time(filter_spec * gated_spec)
    conved = conv_part + skip_gain[:, None] * gated
    output = (post_f * conved).astype(jnp.bfloat16)
    grad_f = cotangent.astype(jnp.float32)
    d_post = (grad_f * conved).astype(jnp.bfloat16)
    d_conved = grad_f * post_f
    d_spec = spectra(d_conved)
    d_gated = to_time(jnp.conj(filter_spec) * d_spec) + skip_gain[:, None] * d_conved
    d_pre = (d_gated * signal_f).astype(jnp.bfloat16)
    d_signal = (d_gated * pre_f).astype(jnp.bfloat16)
    d_filter = to_time(jnp.conj(gated_spec) * d_spec) / (TOKENS ** 0.5)
    d_skip = jnp.sum(d_conved * gated, axis=1) / (TOKENS ** 0.5)
    return output, d_post, d_pre, d_signal, d_skip, d_filter
```

```python
import functools
import math

import jax
import jax.numpy as jnp
import ml_dtypes
import numpy as np
from jax import lax
from jax.experimental import pallas as pl
from jax.experimental.pallas import tpu as pltpu
from jax.sharding import PartitionSpec as P

LANES = 128
SUBLANES = 8
BF16 = jnp.bfloat16
F32 = jnp.float32


def halves(table):
    high = table.astype(np.float32).astype(ml_dtypes.bfloat16)
    low = (table - high.astype(np.float64)).astype(np.float32).astype(ml_dtypes.bfloat16)
    return high, low


def tables(shards_of, total_len):
    blocks = total_len // LANES
    per_shard = blocks // shards_of
    k = np.arange(blocks)[:, None]
    a = np.arange(blocks)[None, :]
    angle = np.pi * (2 * k + 1) * a / (2 * blocks)
    outer = np.concatenate([np.cos(angle), -np.sin(angle)], axis=0)
    inverse = np.concatenate([np.cos(angle).T, -np.sin(angle).T], axis=1) / total_len
    filter_inverse = inverse / math.sqrt(total_len)
    order = [
        np.concatenate(
            [np.arange(per_shard) + (me ^ d) * per_shard for d in range(shards_of)]
        )
        for me in range(shards_of)
    ]

    def wide(table):
        high, low = halves(table)
        return np.concatenate([high, high, low], axis=1)

    outer_w = np.stack([wide(outer[:, o]) for o in order])
    inverse_w = np.stack([wide(inverse[o]) for o in order])
    filter_w = np.stack([wide(filter_inverse[o]) for o in order])
    b = np.arange(LANES)[None, :]
    turn = np.pi * (2 * k + 1) * b / (2 * total_len)
    twiddle = np.stack([np.cos(turn), np.sin(turn)]).astype(np.float32)
    q = np.arange(LANES)
    inner = 2 * np.pi * (q[:, None] * q[None, :] % LANES) / LANES
    dft = np.block([[np.cos(inner), -np.sin(inner)], [np.sin(inner), np.cos(inner)]])
    dft_high, dft_low = halves(dft)
    return outer_w, inverse_w, filter_w, twiddle, np.stack([dft_high, dft_low])


def split(x):
    high = x.astype(BF16)
    low = (x - high.astype(F32)).astype(BF16)
    return high, low


def outer_mix(table, x):
    high, low = split(x)
    return jnp.dot(table, jnp.concatenate([high, low, high], axis=0), preferred_element_type=F32)


def inner_mix(x, dft_ref):
    high, low = split(x)
    return (
        jnp.dot(high, dft_ref[0], preferred_element_type=F32)
        + jnp.dot(low, dft_ref[0], preferred_element_type=F32)
        + jnp.dot(high, dft_ref[1], preferred_element_type=F32)
    )


def pack_kernel(shards_of, post, pre, signal, cotangent, taps, *outs):
    me = lax.axis_index("seq")
    channels, length = post.shape
    group = channels // shards_of
    per = length // LANES
    field_rows = group * per
    for d in range(shards_of):
        rows = pl.ds(pl.multiple_of((me ^ d) * group, group), group)
        gated = pre[rows, :].astype(F32) * signal[rows, :].astype(F32)
        d_conved = cotangent[rows, :].astype(F32) * post[rows, :].astype(F32)
        for f, x in enumerate((taps[rows, :], gated, d_conved)):
            for cb in range(group // SUBLANES):
                for a in range(per):
                    start = f * field_rows + cb * SUBLANES * per + a
                    outs[d][pl.ds(start, SUBLANES, stride=per), :] = x[
                        cb * SUBLANES : (cb + 1) * SUBLANES, a * LANES : (a + 1) * LANES
                    ]
    parts = []
    for cb in range(0, channels, 16):
        prod = (pre[cb : cb + 16, :].astype(F32) * signal[cb : cb + 16, :].astype(F32)) * (
            cotangent[cb : cb + 16, :].astype(F32) * post[cb : cb + 16, :].astype(F32)
        )
        parts.append(sum(prod[:, a * LANES : (a + 1) * LANES] for a in range(per)))
    folded = jnp.concatenate(parts + [jnp.zeros((LANES - channels, LANES), F32)], axis=0)
    skip = jnp.sum(folded.T, axis=0, keepdims=True)
    for d in range(shards_of):
        outs[d][3 * field_rows :, :] = jnp.broadcast_to(skip, (SUBLANES, LANES))


def spectral_kernel(shards_of, group, per, *refs):
    skip_gain, outer_w, inverse_w, filter_w, twiddle, dft = refs[:6]
    pieces = refs[6 : 6 + shards_of]
    outs = refs[6 + shards_of : 6 + 2 * shards_of]
    d_skip = refs[6 + 2 * shards_of]
    spectra = refs[7 + 2 * shards_of :]
    me = lax.axis_index("seq")
    blocks = shards_of * per
    field_rows = group * per
    cos_t = twiddle[0]
    sin_t = twiddle[1]
    forward = outer_w[me]
    first = (lax.broadcasted_iota(jnp.int32, (per, LANES), 0) == 0) & (
        lax.broadcasted_iota(jnp.int32, (per, LANES), 1) == 0
    )
    total_len = blocks * LANES
    skips = sum(pieces[d][3 * field_rows : 3 * field_rows + 1, :] for d in range(shards_of))
    d_skip[...] = skips[:, : d_skip.shape[1]] * (1.0 / math.sqrt(total_len))

    for f in range(3):
        for c in range(0, group, 2):
            cols = []
            for ch in (c, c + 1):
                start = f * field_rows + ch * per
                cols.append(
                    jnp.concatenate([pieces[d][start : start + per, :] for d in range(shards_of)], axis=0)
                )
            mixed = outer_mix(forward, jnp.concatenate(cols, axis=1))
            for i in range(2):
                real = mixed[:blocks, i * LANES : (i + 1) * LANES]
                imag = mixed[blocks:, i * LANES : (i + 1) * LANES]
                row = jnp.concatenate(
                    [real * cos_t + imag * sin_t, imag * cos_t - real * sin_t], axis=1
                )
                spectra[f][pl.ds((c + i) * blocks, blocks), :] = inner_mix(row, dft)
    back = inverse_w[me]
    filter_back = filter_w[me]
    for c in range(0, group, 2):
        pairs = [[], [], []]
        for ch in (c, c + 1):
            rows = pl.ds(ch * blocks, blocks)
            tr, ti = spectra[0][rows, :LANES], spectra[0][rows, LANES:]
            gr, gi = spectra[1][rows, :LANES], spectra[1][rows, LANES:]
            dr, di = spectra[2][rows, :LANES], spectra[2][rows, LANES:]
            tr = tr + skip_gain[me * group + ch]
            products = (
                (gr * tr - gi * ti, gr * ti + gi * tr),
                (tr * dr + ti * di, tr * di - ti * dr),
                (gr * dr + gi * di, gr * di - gi * dr),
            )
            for f in range(3):
                real, imag = products[f]
                swapped = inner_mix(jnp.concatenate([imag, real], axis=1), dft)
                imag, real = swapped[:, :LANES], swapped[:, LANES:]
                pairs[f].append(
                    jnp.concatenate(
                        [real * cos_t - imag * sin_t, imag * cos_t + real * sin_t], axis=0
                    )
                )
        for f in range(3):
            y = outer_mix(filter_back if f == 2 else back, jnp.concatenate(pairs[f], axis=1))
            for i in range(2):
                start = f * field_rows + (c + i) * per
                for d in range(shards_of):
                    outs[d][start : start + per, :] = y[
                        d * per : (d + 1) * per, i * LANES : (i + 1) * LANES
                    ]


def gate_kernel(shards_of, *refs):
    post, pre, signal, cotangent = refs[:4]
    pieces = refs[4 : 4 + shards_of]
    output, d_post, d_pre, d_signal, d_filter = refs[4 + shards_of :]
    me = lax.axis_index("seq")
    channels, length = post.shape
    group = channels // shards_of
    per = length // LANES
    field_rows = group * per
    for d in range(shards_of):
        rows = pl.ds(pl.multiple_of((me ^ d) * group, group), group)
        for a in range(per):
            cols = slice(a * LANES, (a + 1) * LANES)

            def field(f):
                return jnp.concatenate(
                    [
                        pieces[d][pl.ds(f * field_rows + cb * per + a, SUBLANES, stride=per), :]
                        for cb in range(0, group, SUBLANES)
                    ],
                    axis=0,
                )

            conved, d_gated = field(0), field(1)
            output[rows, cols] = (post[rows, cols].astype(F32) * conved).astype(BF16)
            d_post[rows, cols] = (cotangent[rows, cols].astype(F32) * conved).astype(BF16)
            d_pre[rows, cols] = (signal[rows, cols].astype(F32) * d_gated).astype(BF16)
            d_signal[rows, cols] = (pre[rows, cols].astype(F32) * d_gated).astype(BF16)
            d_filter[rows, cols] = field(2)


def shards(post_gate, pre_gate, signal, cotangent, filter_taps, skip_gain):
    shards_of = lax.axis_size("seq")
    channels, length = post_gate.shape
    group = channels // shards_of
    per = length // LANES
    field_rows = group * per
    total_len = shards_of * length
    vmem = pl.BlockSpec(memory_space=pltpu.VMEM)
    params = pltpu.CompilerParams(vmem_limit_bytes=48 * 2**20)

    def swap(pieces):
        return [pieces[0]] + [
            lax.ppermute(pieces[d], "seq", [(i, i ^ d) for i in range(shards_of)])
            for d in range(1, shards_of)
        ]

    packed = pl.pallas_call(
        functools.partial(pack_kernel, shards_of),
        out_shape=[jax.ShapeDtypeStruct((3 * field_rows + SUBLANES, LANES), F32)] * shards_of,
        in_specs=[vmem] * 5,
        out_specs=[vmem] * shards_of,
        compiler_params=params,
    )(post_gate, pre_gate, signal, cotangent, filter_taps)
    packed = swap(packed)
    consts = [jnp.asarray(t) for t in tables(shards_of, total_len)]
    *mixed, d_skip = pl.pallas_call(
        functools.partial(spectral_kernel, shards_of, group, per),
        out_shape=[jax.ShapeDtypeStruct((3 * field_rows, LANES), F32)] * shards_of
        + [jax.ShapeDtypeStruct((1, channels), F32)],
        in_specs=[pl.BlockSpec(memory_space=pltpu.SMEM)] + [vmem] * (5 + shards_of),
        out_specs=[vmem] * (shards_of + 1),
        scratch_shapes=[pltpu.VMEM((group * shards_of * per, 2 * LANES), F32)] * 3,
        compiler_params=params,
    )(skip_gain, *consts, *packed)
    mixed = swap(mixed)
    wide = jax.ShapeDtypeStruct((channels, length), BF16)
    output, d_post, d_pre, d_signal, d_filter = pl.pallas_call(
        functools.partial(gate_kernel, shards_of),
        out_shape=[wide] * 4 + [jax.ShapeDtypeStruct((channels, length), F32)],
        in_specs=[vmem] * (4 + shards_of),
        out_specs=[vmem] * 5,
        compiler_params=params,
    )(post_gate, pre_gate, signal, cotangent, *mixed)
    return (output, d_post, d_pre, d_signal, d_skip.reshape(channels), d_filter)


def solution(mesh):
    both = P("chan", "seq")
    return jax.shard_map(
        shards,
        mesh=mesh,
        in_specs=(both,) * 5 + (P("chan"),),
        out_specs=(both,) * 4 + (P("chan"), both),
        check_vma=False,
    )
```

```python
import functools
import math

import jax
import jax.numpy as jnp
import ml_dtypes
import numpy as np
from jax import lax
from jax.experimental import pallas as pl
from jax.experimental.pallas import tpu as pltpu
from jax.sharding import PartitionSpec as P

LANES = 128
CHUNKS = 1
SUBLANES = 8
BF16 = jnp.bfloat16
F32 = jnp.float32


def halves(table):
    high = table.astype(np.float32).astype(ml_dtypes.bfloat16)
    low = (table - high.astype(np.float64)).astype(np.float32).astype(ml_dtypes.bfloat16)
    return high, low


def tables(shards_of, total_len):
    blocks = total_len // LANES
    per_shard = blocks // shards_of
    k = np.arange(blocks)[:, None]
    a = np.arange(blocks)[None, :]
    angle = np.pi * (2 * k + 1) * a / (2 * blocks)
    outer = np.concatenate([np.cos(angle), -np.sin(angle)], axis=0)
    inverse = np.concatenate([np.cos(angle).T, -np.sin(angle).T], axis=1) / total_len
    filter_inverse = inverse / math.sqrt(total_len)
    order = [
        np.concatenate(
            [np.arange(per_shard) + (me ^ d) * per_shard for d in range(shards_of)]
        )
        for me in range(shards_of)
    ]

    def wide(table):
        high, low = halves(table)
        return np.concatenate([high, high, low], axis=1)

    outer_w = np.stack([wide(outer[:, o]) for o in order])
    inverse_w = np.stack([wide(inverse[o]) for o in order])
    filter_w = np.stack([wide(filter_inverse[o]) for o in order])
    b = np.arange(LANES)[None, :]
    turn = np.pi * (2 * k + 1) * b / (2 * total_len)
    twiddle = np.stack([np.cos(turn), np.sin(turn)]).astype(np.float32)
    q = np.arange(LANES)
    inner = 2 * np.pi * (q[:, None] * q[None, :] % LANES) / LANES
    dft = np.block([[np.cos(inner), -np.sin(inner)], [np.sin(inner), np.cos(inner)]])
    dft_high, dft_low = halves(dft)
    return outer_w, inverse_w, filter_w, twiddle, np.concatenate([dft_high, dft_high, dft_low])


def split(x):
    high = x.astype(BF16)
    low = (x - high.astype(F32)).astype(BF16)
    return high, low


def outer_mix(table, x):
    high, low = split(x)
    return jnp.dot(table, jnp.concatenate([high, low, high], axis=0), preferred_element_type=F32)


def triple(x):
    high, low = split(x)
    return jnp.concatenate([high, low, high], axis=1)


def group_rows(ref, index, group):
    if group % 16 == 0:
        return ref[pl.ds(pl.multiple_of(index * group, 16), group), :].astype(F32)
    pair = ref[pl.ds(pl.multiple_of(index // 2 * 16, 16), 16), :].astype(F32)
    return jnp.where(index % 2 == 0, pair[:SUBLANES], pair[SUBLANES:])


def pack_kernel(shards_of, chunks, *refs):
    sources = refs[:5]
    outs = refs[5 : 5 + chunks * shards_of]
    post, pre, signal, cotangent, taps, sems = refs[5 + chunks * shards_of :]
    copies = [
        pltpu.make_async_copy(source, held, sems.at[i])
        for i, (source, held) in enumerate(zip(sources, (post, pre, signal, cotangent, taps)))
    ]
    for copy in copies:
        copy.start()
    for copy in copies:
        copy.wait()
    me = lax.axis_index("seq")
    channels, length = post.shape
    group = channels // shards_of
    width = group // chunks
    per = length // LANES
    field_rows = width * per
    for d in range(shards_of):
        owner = me ^ d
        gated = group_rows(pre, owner, group) * group_rows(signal, owner, group)
        d_conved = group_rows(cotangent, owner, group) * group_rows(post, owner, group)
        for f, x in enumerate((group_rows(taps, owner, group), gated, d_conved)):
            for q in range(chunks):
                for cb in range(0, width, SUBLANES):
                    for a in range(per):
                        start = f * field_rows + cb * per + a
                        top = q * width + cb
                        outs[q * shards_of + d][pl.ds(start, SUBLANES, stride=per), :] = x[
                            top : top + SUBLANES, a * LANES : (a + 1) * LANES
                        ]
    parts = []
    for cb in range(0, channels, 16):
        prod = (pre[cb : cb + 16, :].astype(F32) * signal[cb : cb + 16, :].astype(F32)) * (
            cotangent[cb : cb + 16, :].astype(F32) * post[cb : cb + 16, :].astype(F32)
        )
        parts.append(sum(prod[:, a * LANES : (a + 1) * LANES] for a in range(per)))
    folded = jnp.concatenate(parts + [jnp.zeros((LANES - channels, LANES), F32)], axis=0)
    skip = jnp.sum(folded.T, axis=0, keepdims=True)
    for d in range(shards_of):
        outs[d][3 * field_rows :, :] = jnp.broadcast_to(skip, (SUBLANES, LANES))


def spectral_kernel(shards_of, chunks, q, group, per, *refs):
    skip_gain, outer_w, inverse_w, filter_w, twiddle, dft = refs[:6]
    pieces = refs[6 : 6 + shards_of]
    outs = refs[6 + shards_of : 6 + 2 * shards_of]
    rest = refs[6 + 2 * shards_of :]
    if q == 0:
        d_skip, *rest = rest
    spectra, packed = rest[:3], rest[3:]
    width = group // chunks
    me = lax.axis_index("seq")
    blocks = shards_of * per
    field_rows = width * per
    cos_t = twiddle[0]
    sin_t = twiddle[1]
    forward = outer_w[me]
    total_len = blocks * LANES
    if q == 0:
        skips = sum(pieces[d][3 * field_rows : 3 * field_rows + 1, :] for d in range(shards_of))
        d_skip[...] = skips[:, : d_skip.shape[1]] * (1.0 / math.sqrt(total_len))

    for f in range(3):
        for c in range(0, width, 2):
            cols = []
            for ch in (c, c + 1):
                start = f * field_rows + ch * per
                cols.append(
                    jnp.concatenate([pieces[d][start : start + per, :] for d in range(shards_of)], axis=0)
                )
            mixed = outer_mix(forward, jnp.concatenate(cols, axis=1))
            for i in range(2):
                real = mixed[:blocks, i * LANES : (i + 1) * LANES]
                imag = mixed[blocks:, i * LANES : (i + 1) * LANES]
                row = jnp.concatenate(
                    [real * cos_t + imag * sin_t, imag * cos_t - real * sin_t], axis=1
                )
                packed[f][pl.ds((c + i) * blocks, blocks), :] = triple(row)
        spectra[f][...] = jnp.dot(packed[f][...], dft[...], preferred_element_type=F32)
    back = inverse_w[me]
    filter_back = filter_w[me]
    for ch in range(width):
        rows = pl.ds(ch * blocks, blocks)
        tr, ti = spectra[0][rows, :LANES], spectra[0][rows, LANES:]
        gr, gi = spectra[1][rows, :LANES], spectra[1][rows, LANES:]
        dr, di = spectra[2][rows, :LANES], spectra[2][rows, LANES:]
        tr = tr + skip_gain[me * group + q * width + ch]
        products = (
            (gr * tr - gi * ti, gr * ti + gi * tr),
            (tr * dr + ti * di, tr * di - ti * dr),
            (gr * dr + gi * di, gr * di - gi * dr),
        )
        for f, (real, imag) in enumerate(products):
            packed[f][rows, :] = triple(jnp.concatenate([imag, real], axis=1))
    for f in range(3):
        spectra[f][...] = jnp.dot(packed[f][...], dft[...], preferred_element_type=F32)
        for c in range(0, width, 2):
            cols = []
            for ch in (c, c + 1):
                rows = pl.ds(ch * blocks, blocks)
                imag, real = spectra[f][rows, :LANES], spectra[f][rows, LANES:]
                cols.append(
                    jnp.concatenate(
                        [real * cos_t - imag * sin_t, imag * cos_t + real * sin_t], axis=0
                    )
                )
            y = outer_mix(filter_back if f == 2 else back, jnp.concatenate(cols, axis=1))
            for i in range(2):
                start = f * field_rows + (c + i) * per
                for d in range(shards_of):
                    outs[d][start : start + per, :] = y[
                        d * per : (d + 1) * per, i * LANES : (i + 1) * LANES
                    ]


def gate_kernel(shards_of, chunks, *refs):
    post, pre, signal, cotangent = refs[:4]
    pieces = refs[4 : 4 + chunks * shards_of]
    output, d_post, d_pre, d_signal, d_filter = refs[4 + chunks * shards_of :]
    me = lax.axis_index("seq")
    channels, length = post.shape
    group = channels // shards_of
    per = length // LANES
    width = group // chunks
    field_rows = width * per
    for d in range(shards_of):
        rows = pl.ds(pl.multiple_of((me ^ d) * group, group), group)
        for a in range(per):
            cols = slice(a * LANES, (a + 1) * LANES)

            def field(f):
                return jnp.concatenate(
                    [
                        pieces[q * shards_of + d][
                            pl.ds(f * field_rows + cb * per + a, SUBLANES, stride=per), :
                        ]
                        for q in range(chunks)
                        for cb in range(0, width, SUBLANES)
                    ],
                    axis=0,
                )

            conved, d_gated = field(0), field(1)
            output[rows, cols] = (post[rows, cols].astype(F32) * conved).astype(BF16)
            d_post[rows, cols] = (cotangent[rows, cols].astype(F32) * conved).astype(BF16)
            d_pre[rows, cols] = (signal[rows, cols].astype(F32) * d_gated).astype(BF16)
            d_signal[rows, cols] = (pre[rows, cols].astype(F32) * d_gated).astype(BF16)
            d_filter[rows, cols] = field(2)


def shards(post_gate, pre_gate, signal, cotangent, filter_taps, skip_gain):
    shards_of = lax.axis_size("seq")
    channels, length = post_gate.shape
    group = channels // shards_of
    per = length // LANES
    chunks = CHUNKS if group % (CHUNKS * SUBLANES) == 0 else 1
    width = group // chunks
    field_rows = width * per
    total_len = shards_of * length
    vmem = pl.BlockSpec(memory_space=pltpu.VMEM)
    params = pltpu.CompilerParams(vmem_limit_bytes=48 * 2**20)

    def swap(pieces):
        moved = {
            d: lax.ppermute(pieces[d], "seq", [(i, i ^ d) for i in range(shards_of)])
            for d in reversed(range(1, shards_of))
        }
        return [pieces[0]] + [moved[d] for d in range(1, shards_of)]

    def rows(count):
        return [jax.ShapeDtypeStruct((count, LANES), F32)] * shards_of

    packed = pl.pallas_call(
        functools.partial(pack_kernel, shards_of, chunks),
        out_shape=rows(3 * field_rows + SUBLANES) + rows(3 * field_rows) * (chunks - 1),
        in_specs=[pl.BlockSpec(memory_space=pltpu.HBM)] * 5,
        out_specs=[vmem] * (chunks * shards_of),
        scratch_shapes=[pltpu.VMEM((channels, length), BF16)] * 4
        + [pltpu.VMEM((channels, length), F32), pltpu.SemaphoreType.DMA((5,))],
        compiler_params=params,
    )(
        *(
            pltpu.with_memory_space_constraint(x, pltpu.HBM)
            for x in (post_gate, pre_gate, signal, cotangent, filter_taps)
        )
    )
    arrived = [swap(packed[q * shards_of : (q + 1) * shards_of]) for q in range(chunks)]
    consts = [jnp.asarray(t) for t in tables(shards_of, total_len)]
    spectrum_rows = width * shards_of * per
    mixed = []
    for q in range(chunks):
        out = pl.pallas_call(
            functools.partial(spectral_kernel, shards_of, chunks, q, group, per),
            out_shape=rows(3 * field_rows)
            + [jax.ShapeDtypeStruct((1, channels), F32)] * (q == 0),
            in_specs=[pl.BlockSpec(memory_space=pltpu.SMEM)] + [vmem] * (5 + shards_of),
            out_specs=[vmem] * (shards_of + (q == 0)),
            scratch_shapes=[pltpu.VMEM((spectrum_rows, 2 * LANES), F32)] * 3
            + [pltpu.VMEM((spectrum_rows, 6 * LANES), BF16)] * 3,
            compiler_params=params,
        )(skip_gain, *consts, *arrived[q])
        if q == 0:
            d_skip = out[shards_of]
        mixed += swap(out[:shards_of])
    wide = jax.ShapeDtypeStruct((channels, length), BF16)
    output, d_post, d_pre, d_signal, d_filter = pl.pallas_call(
        functools.partial(gate_kernel, shards_of, chunks),
        out_shape=[wide] * 4 + [jax.ShapeDtypeStruct((channels, length), F32)],
        in_specs=[vmem] * (4 + chunks * shards_of),
        out_specs=[vmem] * 5,
        compiler_params=params,
    )(post_gate, pre_gate, signal, cotangent, *mixed)
    return (output, d_post, d_pre, d_signal, d_skip.reshape(channels), d_filter)


def solution(mesh):
    both = P("chan", "seq")
    return jax.shard_map(
        shards,
        mesh=mesh,
        in_specs=(both,) * 5 + (P("chan"),),
        out_specs=(both,) * 4 + (P("chan"), both),
        check_vma=False,
    )
```

```python
import functools
import math

import jax
import jax.numpy as jnp
import ml_dtypes
import numpy as np
from jax import lax
from jax.experimental import pallas as pl
from jax.experimental.pallas import tpu as pltpu
from jax.sharding import PartitionSpec as P

LANES = 128
CHUNKS = 2
SUBLANES = 8
BF16 = jnp.bfloat16
F32 = jnp.float32


def halves(table):
    high = table.astype(np.float32).astype(ml_dtypes.bfloat16)
    low = (table - high.astype(np.float64)).astype(np.float32).astype(ml_dtypes.bfloat16)
    return high, low


def tables(shards_of, total_len):
    blocks = total_len // LANES
    per_shard = blocks // shards_of
    k = np.arange(blocks)[:, None]
    a = np.arange(blocks)[None, :]
    angle = np.pi * (2 * k + 1) * a / (2 * blocks)
    outer = np.concatenate([np.cos(angle), -np.sin(angle)], axis=0)
    inverse = np.concatenate([np.cos(angle).T, -np.sin(angle).T], axis=1) / total_len
    filter_inverse = inverse / math.sqrt(total_len)
    order = [
        np.concatenate(
            [np.arange(per_shard) + (me ^ d) * per_shard for d in range(shards_of)]
        )
        for me in range(shards_of)
    ]

    def wide(table):
        high, low = halves(table)
        return np.concatenate([high, high, low], axis=1)

    outer_w = np.stack([wide(outer[:, o]) for o in order])
    inverse_w = np.stack([wide(inverse[o]) for o in order])
    filter_w = np.stack([wide(filter_inverse[o]) for o in order])
    b = np.arange(LANES)[None, :]
    turn = np.pi * (2 * k + 1) * b / (2 * total_len)
    twiddle = np.stack([np.cos(turn), np.sin(turn)]).astype(np.float32)
    q = np.arange(LANES)
    inner = 2 * np.pi * (q[:, None] * q[None, :] % LANES) / LANES
    dft = np.block([[np.cos(inner), -np.sin(inner)], [np.sin(inner), np.cos(inner)]])
    dft_high, dft_low = halves(dft)
    return outer_w, inverse_w, filter_w, twiddle, np.concatenate([dft_high, dft_high, dft_low])


def split(x):
    high = x.astype(BF16)
    low = (x - high.astype(F32)).astype(BF16)
    return high, low


def outer_mix(table, x):
    high, low = split(x)
    return jnp.dot(table, jnp.concatenate([high, low, high], axis=0), preferred_element_type=F32)


def triple(x):
    high, low = split(x)
    return jnp.concatenate([high, low, high], axis=1)


def group_rows(ref, index, group):
    if group % 16 == 0:
        return ref[pl.ds(pl.multiple_of(index * group, 16), group), :].astype(F32)
    pair = ref[pl.ds(pl.multiple_of(index // 2 * 16, 16), 16), :].astype(F32)
    return jnp.where(index % 2 == 0, pair[:SUBLANES], pair[SUBLANES:])


def pack_kernel(shards_of, chunks, *refs):
    sources = refs[:5]
    outs = refs[5 : 5 + chunks * shards_of]
    post, pre, signal, cotangent, taps, sems = refs[5 + chunks * shards_of :]
    copies = [
        pltpu.make_async_copy(source, held, sems.at[i])
        for i, (source, held) in enumerate(zip(sources, (post, pre, signal, cotangent, taps)))
    ]
    for copy in copies:
        copy.start()
    for copy in copies:
        copy.wait()
    me = lax.axis_index("seq")
    channels, length = post.shape
    group = channels // shards_of
    width = group // chunks
    per = length // LANES
    field_rows = width * per
    for d in range(shards_of):
        owner = me ^ d
        gated = group_rows(pre, owner, group) * group_rows(signal, owner, group)
        d_conved = group_rows(cotangent, owner, group) * group_rows(post, owner, group)
        for f, x in enumerate((group_rows(taps, owner, group), gated, d_conved)):
            for q in range(chunks):
                for cb in range(0, width, SUBLANES):
                    for a in range(per):
                        start = f * field_rows + cb * per + a
                        top = q * width + cb
                        outs[q * shards_of + d][pl.ds(start, SUBLANES, stride=per), :] = x[
                            top : top + SUBLANES, a * LANES : (a + 1) * LANES
                        ]
    parts = []
    for cb in range(0, channels, 16):
        prod = (pre[cb : cb + 16, :].astype(F32) * signal[cb : cb + 16, :].astype(F32)) * (
            cotangent[cb : cb + 16, :].astype(F32) * post[cb : cb + 16, :].astype(F32)
        )
        parts.append(sum(prod[:, a * LANES : (a + 1) * LANES] for a in range(per)))
    folded = jnp.concatenate(parts + [jnp.zeros((LANES - channels, LANES), F32)], axis=0)
    skip = jnp.sum(folded.T, axis=0, keepdims=True)
    for d in range(shards_of):
        outs[d][3 * field_rows :, :] = jnp.broadcast_to(skip, (SUBLANES, LANES))


def spectral_kernel(shards_of, chunks, q, group, per, *refs):
    skip_gain, outer_w, inverse_w, filter_w, twiddle, dft = refs[:6]
    pieces = refs[6 : 6 + shards_of]
    outs = refs[6 + shards_of : 6 + 2 * shards_of]
    rest = refs[6 + 2 * shards_of :]
    if q == 0:
        d_skip, *rest = rest
    spectra, packed = rest[:3], rest[3:]
    width = group // chunks
    me = lax.axis_index("seq")
    blocks = shards_of * per
    field_rows = width * per
    cos_t = twiddle[0]
    sin_t = twiddle[1]
    forward = outer_w[me]
    total_len = blocks * LANES
    if q == 0:
        skips = sum(pieces[d][3 * field_rows : 3 * field_rows + 1, :] for d in range(shards_of))
        d_skip[...] = skips[:, : d_skip.shape[1]] * (1.0 / math.sqrt(total_len))

    for f in range(3):
        for c in range(0, width, 2):
            cols = []
            for ch in (c, c + 1):
                start = f * field_rows + ch * per
                cols.append(
                    jnp.concatenate([pieces[d][start : start + per, :] for d in range(shards_of)], axis=0)
                )
            mixed = outer_mix(forward, jnp.concatenate(cols, axis=1))
            for i in range(2):
                real = mixed[:blocks, i * LANES : (i + 1) * LANES]
                imag = mixed[blocks:, i * LANES : (i + 1) * LANES]
                row = jnp.concatenate(
                    [real * cos_t + imag * sin_t, imag * cos_t - real * sin_t], axis=1
                )
                packed[f][pl.ds((c + i) * blocks, blocks), :] = triple(row)
        spectra[f][...] = jnp.dot(packed[f][...], dft[...], preferred_element_type=F32)
    back = inverse_w[me]
    filter_back = filter_w[me]
    for ch in range(width):
        rows = pl.ds(ch * blocks, blocks)
        tr, ti = spectra[0][rows, :LANES], spectra[0][rows, LANES:]
        gr, gi = spectra[1][rows, :LANES], spectra[1][rows, LANES:]
        dr, di = spectra[2][rows, :LANES], spectra[2][rows, LANES:]
        tr = tr + skip_gain[me * group + q * width + ch]
        products = (
            (gr * tr - gi * ti, gr * ti + gi * tr),
            (tr * dr + ti * di, tr * di - ti * dr),
            (gr * dr + gi * di, gr * di - gi * dr),
        )
        for f, (real, imag) in enumerate(products):
            packed[f][rows, :] = triple(jnp.concatenate([imag, real], axis=1))
    for f in range(3):
        spectra[f][...] = jnp.dot(packed[f][...], dft[...], preferred_element_type=F32)
        for c in range(0, width, 2):
            cols = []
            for ch in (c, c + 1):
                rows = pl.ds(ch * blocks, blocks)
                imag, real = spectra[f][rows, :LANES], spectra[f][rows, LANES:]
                cols.append(
                    jnp.concatenate(
                        [real * cos_t - imag * sin_t, imag * cos_t + real * sin_t], axis=0
                    )
                )
            y = outer_mix(filter_back if f == 2 else back, jnp.concatenate(cols, axis=1))
            for i in range(2):
                start = f * field_rows + (c + i) * per
                for d in range(shards_of):
                    outs[d][start : start + per, :] = y[
                        d * per : (d + 1) * per, i * LANES : (i + 1) * LANES
                    ]


def gate_kernel(shards_of, chunks, *refs):
    post, pre, signal, cotangent = refs[:4]
    pieces = refs[4 : 4 + chunks * shards_of]
    output, d_post, d_pre, d_signal, d_filter = refs[4 + chunks * shards_of :]
    me = lax.axis_index("seq")
    channels, length = post.shape
    group = channels // shards_of
    per = length // LANES
    width = group // chunks
    field_rows = width * per
    for d in range(shards_of):
        rows = pl.ds(pl.multiple_of((me ^ d) * group, group), group)
        for a in range(per):
            cols = slice(a * LANES, (a + 1) * LANES)

            def field(f):
                return jnp.concatenate(
                    [
                        pieces[q * shards_of + d][
                            pl.ds(f * field_rows + cb * per + a, SUBLANES, stride=per), :
                        ]
                        for q in range(chunks)
                        for cb in range(0, width, SUBLANES)
                    ],
                    axis=0,
                )

            conved, d_gated = field(0), field(1)
            output[rows, cols] = (post[rows, cols].astype(F32) * conved).astype(BF16)
            d_post[rows, cols] = (cotangent[rows, cols].astype(F32) * conved).astype(BF16)
            d_pre[rows, cols] = (signal[rows, cols].astype(F32) * d_gated).astype(BF16)
            d_signal[rows, cols] = (pre[rows, cols].astype(F32) * d_gated).astype(BF16)
            d_filter[rows, cols] = field(2)


def shards(post_gate, pre_gate, signal, cotangent, filter_taps, skip_gain):
    shards_of = lax.axis_size("seq")
    channels, length = post_gate.shape
    group = channels // shards_of
    per = length // LANES
    chunks = CHUNKS if group % (CHUNKS * SUBLANES) == 0 else 1
    width = group // chunks
    field_rows = width * per
    total_len = shards_of * length
    vmem = pl.BlockSpec(memory_space=pltpu.VMEM)
    params = pltpu.CompilerParams(vmem_limit_bytes=48 * 2**20)

    def swap(pieces):
        moved = {
            d: lax.ppermute(pieces[d], "seq", [(i, i ^ d) for i in range(shards_of)])
            for d in reversed(range(1, shards_of))
        }
        return [pieces[0]] + [moved[d] for d in range(1, shards_of)]

    def rows(count):
        return [jax.ShapeDtypeStruct((count, LANES), F32)] * shards_of

    packed = pl.pallas_call(
        functools.partial(pack_kernel, shards_of, chunks),
        out_shape=rows(3 * field_rows + SUBLANES) + rows(3 * field_rows) * (chunks - 1),
        in_specs=[pl.BlockSpec(memory_space=pltpu.HBM)] * 5,
        out_specs=[vmem] * (chunks * shards_of),
        scratch_shapes=[pltpu.VMEM((channels, length), BF16)] * 4
        + [pltpu.VMEM((channels, length), F32), pltpu.SemaphoreType.DMA((5,))],
        compiler_params=params,
    )(
        *(
            pltpu.with_memory_space_constraint(x, pltpu.HBM)
            for x in (post_gate, pre_gate, signal, cotangent, filter_taps)
        )
    )
    arrived = [swap(packed[q * shards_of : (q + 1) * shards_of]) for q in range(chunks)]
    consts = [jnp.asarray(t) for t in tables(shards_of, total_len)]
    spectrum_rows = width * shards_of * per
    mixed = []
    for q in range(chunks):
        out = pl.pallas_call(
            functools.partial(spectral_kernel, shards_of, chunks, q, group, per),
            out_shape=rows(3 * field_rows)
            + [jax.ShapeDtypeStruct((1, channels), F32)] * (q == 0),
            in_specs=[pl.BlockSpec(memory_space=pltpu.SMEM)] + [vmem] * (5 + shards_of),
            out_specs=[vmem] * (shards_of + (q == 0)),
            scratch_shapes=[pltpu.VMEM((spectrum_rows, 2 * LANES), F32)] * 3
            + [pltpu.VMEM((spectrum_rows, 6 * LANES), BF16)] * 3,
            compiler_params=params,
        )(skip_gain, *consts, *arrived[q])
        if q == 0:
            d_skip = out[shards_of]
        mixed += swap(out[:shards_of])
    wide = jax.ShapeDtypeStruct((channels, length), BF16)
    output, d_post, d_pre, d_signal, d_filter = pl.pallas_call(
        functools.partial(gate_kernel, shards_of, chunks),
        out_shape=[wide] * 4 + [jax.ShapeDtypeStruct((channels, length), F32)],
        in_specs=[vmem] * (4 + chunks * shards_of),
        out_specs=[vmem] * 5,
        compiler_params=params,
    )(post_gate, pre_gate, signal, cotangent, *mixed)
    return (output, d_post, d_pre, d_signal, d_skip.reshape(channels), d_filter)


def solution(mesh):
    both = P("chan", "seq")
    return jax.shard_map(
        shards,
        mesh=mesh,
        in_specs=(both,) * 5 + (P("chan"),),
        out_specs=(both,) * 4 + (P("chan"), both),
        check_vma=False,
    )
```

```python
import functools
import math

import jax
import jax.numpy as jnp
import ml_dtypes
import numpy as np
from jax import lax
from jax.experimental import pallas as pl
from jax.experimental.pallas import tpu as pltpu
from jax.sharding import PartitionSpec as P

LANES = 128
SUBLANES = 8
CHUNKS = 2
BF16 = jnp.bfloat16
F32 = jnp.float32


def halves(table):
    high = table.astype(np.float32).astype(ml_dtypes.bfloat16)
    low = (table - high.astype(np.float64)).astype(np.float32).astype(ml_dtypes.bfloat16)
    return high, low


def tables(shards_of, total_len):
    blocks = total_len // LANES
    per_shard = blocks // shards_of
    k = np.arange(blocks)[:, None]
    a = np.arange(blocks)[None, :]
    angle = np.pi * (2 * k + 1) * a / (2 * blocks)
    outer = np.concatenate([np.cos(angle), -np.sin(angle)], axis=0)
    inverse = np.concatenate([np.cos(angle).T, -np.sin(angle).T], axis=1) / total_len
    filter_inverse = inverse / math.sqrt(total_len)
    order = [
        np.concatenate(
            [np.arange(per_shard) + (me ^ d) * per_shard for d in range(shards_of)]
        )
        for me in range(shards_of)
    ]

    def wide(table):
        high, low = halves(table)
        return np.concatenate([high, high, low], axis=1)

    outer_w = np.stack([wide(outer[:, o]) for o in order])
    inverse_w = np.stack([wide(inverse[o]) for o in order])
    filter_w = np.stack([wide(filter_inverse[o]) for o in order])
    b = np.arange(LANES)[None, :]
    turn = np.pi * (2 * k + 1) * b / (2 * total_len)
    twiddle = np.stack([np.cos(turn), np.sin(turn)]).astype(np.float32)
    q = np.arange(LANES)
    inner = 2 * np.pi * (q[:, None] * q[None, :] % LANES) / LANES
    dft = np.block([[np.cos(inner), -np.sin(inner)], [np.sin(inner), np.cos(inner)]])
    dft_high, dft_low = halves(dft)
    return outer_w, inverse_w, filter_w, twiddle, np.concatenate([dft_high, dft_high, dft_low])


def triple(x, axis):
    high = x.astype(BF16)
    low = (x - high.astype(F32)).astype(BF16)
    return jnp.concatenate([high, low, high], axis=axis)


def matmul(a, b):
    return jnp.dot(a, b, preferred_element_type=F32)


def pack_kernel(shards_of, chunks, *refs):
    sources = refs[:5]
    outs = refs[5 : 5 + chunks * shards_of]
    post, pre, signal, cotangent, taps, gated, d_conved, sems = refs[5 + chunks * shards_of :]
    copies = [
        pltpu.make_async_copy(source, held, sems.at[i])
        for i, (source, held) in enumerate(zip(sources, (post, pre, signal, cotangent, taps)))
    ]
    for copy in copies:
        copy.start()
    for copy in copies:
        copy.wait()
    me = lax.axis_index("seq")
    channels, length = post.shape
    chunk_rows = channels // chunks
    width = chunk_rows // shards_of
    per = length // LANES
    field_rows = width * per
    parts = []
    for c in range(0, channels, 16):
        rows = slice(c, c + 16)
        g = pre[rows, :].astype(F32) * signal[rows, :].astype(F32)
        dc = cotangent[rows, :].astype(F32) * post[rows, :].astype(F32)
        gated[rows, :] = g
        d_conved[rows, :] = dc
        prod = g * dc
        parts.append(sum(prod[:, a * LANES : (a + 1) * LANES] for a in range(per)))
    folded = jnp.concatenate(parts + [jnp.zeros((LANES - channels, LANES), F32)], axis=0)
    skip = jnp.sum(folded.T, axis=0, keepdims=True)
    for q in range(chunks):
        for d in range(shards_of):
            out = outs[q * shards_of + d]
            top = q * chunk_rows + (me ^ d) * width
            for f, field in enumerate((taps, gated, d_conved)):
                for c in range(0, width, SUBLANES):
                    rows = pl.ds(pl.multiple_of(top + c, SUBLANES), SUBLANES)
                    for a in range(per):
                        out[pl.ds(f * field_rows + c * per + a, SUBLANES, stride=per), :] = field[
                            rows, a * LANES : (a + 1) * LANES
                        ]
            if q == 0:
                out[3 * field_rows :, :] = jnp.broadcast_to(skip, (SUBLANES, LANES))


def spectral_kernel(shards_of, chunks, q, channels, per, *refs):
    skip_gain, outer_w, inverse_w, filter_w, twiddle, dft = refs[:6]
    pieces = refs[6 : 6 + shards_of]
    outs = refs[6 + shards_of : 6 + 2 * shards_of]
    rest = refs[6 + 2 * shards_of :]
    if q == 0:
        d_skip, *rest = rest
    spectra, packed = rest
    me = lax.axis_index("seq")
    chunk_rows = channels // chunks
    width = chunk_rows // shards_of
    blocks = shards_of * per
    field_rows = width * per
    spectrum_rows = width * blocks
    cos_t = twiddle[0]
    sin_t = twiddle[1]
    forward = outer_w[me]
    back = (inverse_w[me], inverse_w[me], filter_w[me])
    if q == 0:
        skips = sum(pieces[d][3 * field_rows : 3 * field_rows + 1, :] for d in range(shards_of))
        d_skip[...] = skips[:, : d_skip.shape[1]] * (1.0 / math.sqrt(blocks * LANES))

    def held(f, ch):
        start = f * field_rows + ch * per
        return jnp.concatenate([pieces[d][start : start + per, :] for d in range(shards_of)], axis=0)

    def spectrum(f, ch):
        start = f * spectrum_rows + ch * blocks
        return slice(start, start + blocks)

    def inner(f):
        rows = slice(f * spectrum_rows, (f + 1) * spectrum_rows)
        spectra[rows, :] = matmul(packed[rows, :], dft[...])

    for f in range(3):
        for c in range(0, width, 2):
            x = jnp.concatenate([held(f, c), held(f, c + 1)], axis=1)
            mixed = matmul(forward, triple(x, 0))
            for i in range(2):
                real = mixed[:blocks, i * LANES : (i + 1) * LANES]
                imag = mixed[blocks:, i * LANES : (i + 1) * LANES]
                turned = [real * cos_t + imag * sin_t, imag * cos_t - real * sin_t]
                packed[spectrum(f, c + i), :] = triple(jnp.concatenate(turned, axis=1), 1)
    for f in range(3):
        inner(f)
    for ch in range(width):
        tr, ti = spectra[spectrum(0, ch), :LANES], spectra[spectrum(0, ch), LANES:]
        gr, gi = spectra[spectrum(1, ch), :LANES], spectra[spectrum(1, ch), LANES:]
        dr, di = spectra[spectrum(2, ch), :LANES], spectra[spectrum(2, ch), LANES:]
        tr = tr + skip_gain[q * chunk_rows + me * width + ch]
        products = (
            (gr * tr - gi * ti, gr * ti + gi * tr),
            (tr * dr + ti * di, tr * di - ti * dr),
            (gr * dr + gi * di, gr * di - gi * dr),
        )
        for f, (real, imag) in enumerate(products):
            packed[spectrum(f, ch), :] = triple(jnp.concatenate([imag, real], axis=1), 1)
    for f in range(3):
        inner(f)
    for f in range(3):
        for c in range(0, width, 2):
            turned = []
            for ch in (c, c + 1):
                imag, real = spectra[spectrum(f, ch), :LANES], spectra[spectrum(f, ch), LANES:]
                both = [real * cos_t - imag * sin_t, imag * cos_t + real * sin_t]
                turned.append(jnp.concatenate(both, axis=0))
            y = matmul(back[f], triple(jnp.concatenate(turned, axis=1), 0))
            for i in range(2):
                start = f * field_rows + (c + i) * per
                for d in range(shards_of):
                    outs[d][start : start + per, :] = y[
                        d * per : (d + 1) * per, i * LANES : (i + 1) * LANES
                    ]


def gate_kernel(shards_of, chunks, *refs):
    post, pre, signal, cotangent = refs[:4]
    pieces = refs[4 : 4 + chunks * shards_of]
    refs = refs[4 + chunks * shards_of :]
    outs, (fields, output, d_post, d_pre, d_signal, sems) = refs[:5], refs[5:]
    me = lax.axis_index("seq")
    channels, length = post.shape
    chunk_rows = channels // chunks
    width = chunk_rows // shards_of
    per = length // LANES
    field_rows = width * per
    copies = []

    def ship(q, i, held):
        rows = pl.ds(q * chunk_rows, chunk_rows)
        copy = pltpu.make_async_copy(held.at[rows, :], outs[i].at[rows, :], sems.at[q, i])
        copy.start()
        copies.append(copy)

    def gather(q, f):
        for d in range(shards_of):
            for c in range(0, width, SUBLANES):
                top = q * chunk_rows + (me ^ d) * width + c
                held = pl.ds(pl.multiple_of(top, SUBLANES), SUBLANES)
                for a in range(per):
                    fields[f, held, a * LANES : (a + 1) * LANES] = pieces[q * shards_of + d][
                        pl.ds(f * field_rows + c * per + a, SUBLANES, stride=per), :
                    ]

    for q in range(chunks):
        rows = slice(q * chunk_rows, (q + 1) * chunk_rows)
        gather(q, 2)
        ship(q, 4, fields.at[2])
        gather(q, 0)
        conved = fields[0, rows, :]
        output[rows, :] = (post[rows, :].astype(F32) * conved).astype(BF16)
        ship(q, 0, output)
        d_post[rows, :] = (cotangent[rows, :].astype(F32) * conved).astype(BF16)
        ship(q, 1, d_post)
        gather(q, 1)
        d_gated = fields[1, rows, :]
        d_pre[rows, :] = (signal[rows, :].astype(F32) * d_gated).astype(BF16)
        ship(q, 2, d_pre)
        d_signal[rows, :] = (pre[rows, :].astype(F32) * d_gated).astype(BF16)
        ship(q, 3, d_signal)
    for copy in copies:
        copy.wait()


def shards(post_gate, pre_gate, signal, cotangent, filter_taps, skip_gain):
    shards_of = lax.axis_size("seq")
    channels, length = post_gate.shape
    chunks = CHUNKS if channels % (CHUNKS * shards_of * SUBLANES) == 0 else 1
    chunk_rows = channels // chunks
    width = chunk_rows // shards_of
    per = length // LANES
    field_rows = width * per
    total_len = shards_of * length
    vmem = pl.BlockSpec(memory_space=pltpu.VMEM)
    hbm = pl.BlockSpec(memory_space=pltpu.HBM)
    params = pltpu.CompilerParams(vmem_limit_bytes=48 * 2**20)

    def swap(pieces):
        moved = {
            d: lax.ppermute(pieces[d], "seq", [(i, i ^ d) for i in range(shards_of)])
            for d in reversed(range(1, shards_of))
        }
        return [pieces[0]] + [moved[d] for d in range(1, shards_of)]

    def rows(count):
        return [jax.ShapeDtypeStruct((count, LANES), F32)] * shards_of

    packed = pl.pallas_call(
        functools.partial(pack_kernel, shards_of, chunks),
        out_shape=rows(3 * field_rows + SUBLANES) + rows(3 * field_rows) * (chunks - 1),
        in_specs=[hbm] * 5,
        out_specs=[vmem] * (chunks * shards_of),
        scratch_shapes=[pltpu.VMEM((channels, length), BF16)] * 4
        + [pltpu.VMEM((channels, length), F32)] * 3
        + [pltpu.SemaphoreType.DMA((5,))],
        compiler_params=params,
    )(
        *(
            pltpu.with_memory_space_constraint(x, pltpu.HBM)
            for x in (post_gate, pre_gate, signal, cotangent, filter_taps)
        )
    )
    arrived = [swap(packed[q * shards_of : (q + 1) * shards_of]) for q in range(chunks)]
    consts = [jnp.asarray(t) for t in tables(shards_of, total_len)]
    spectrum_rows = width * shards_of * per
    back = []
    for q in range(chunks):
        mixed = pl.pallas_call(
            functools.partial(spectral_kernel, shards_of, chunks, q, channels, per),
            out_shape=rows(3 * field_rows)
            + [jax.ShapeDtypeStruct((1, channels), F32)] * (q == 0),
            in_specs=[pl.BlockSpec(memory_space=pltpu.SMEM)] + [vmem] * (5 + shards_of),
            out_specs=[vmem] * (shards_of + (q == 0)),
            scratch_shapes=[
                pltpu.VMEM((3 * spectrum_rows, 2 * LANES), F32),
                pltpu.VMEM((3 * spectrum_rows, 6 * LANES), BF16),
            ],
            compiler_params=params,
        )(skip_gain, *consts, *arrived[q])
        if q == 0:
            d_skip = mixed[shards_of]
        back += swap(mixed[:shards_of])
    output, d_post, d_pre, d_signal, d_filter = pl.pallas_call(
        functools.partial(gate_kernel, shards_of, chunks),
        out_shape=[pltpu.HBM((channels, length), BF16)] * 4 + [pltpu.HBM((channels, length), F32)],
        in_specs=[vmem] * (4 + chunks * shards_of),
        out_specs=[hbm] * 5,
        scratch_shapes=[pltpu.VMEM((3, channels, length), F32)]
        + [pltpu.VMEM((channels, length), BF16)] * 4
        + [pltpu.SemaphoreType.DMA((chunks, 5))],
        compiler_params=params,
    )(post_gate, pre_gate, signal, cotangent, *back)
    return (output, d_post, d_pre, d_signal, d_skip.reshape(channels), d_filter)


def solution(mesh):
    both = P("chan", "seq")
    return jax.shard_map(
        shards,
        mesh=mesh,
        in_specs=(both,) * 5 + (P("chan"),),
        out_specs=(both,) * 4 + (P("chan"), both),
        check_vma=False,
    )
```

```python
import functools
import math

import jax
import jax.numpy as jnp
import ml_dtypes
import numpy as np
from jax import lax
from jax.experimental import pallas as pl
from jax.experimental.pallas import tpu as pltpu
from jax.sharding import PartitionSpec as P

LANES = 128
SUBLANES = 8
CHUNKS = 2
BF16 = jnp.bfloat16
F32 = jnp.float32


def halves(table):
    high = table.astype(np.float32).astype(ml_dtypes.bfloat16)
    low = (table - high.astype(np.float64)).astype(np.float32).astype(ml_dtypes.bfloat16)
    return high, low


def tables(shards_of, total_len):
    blocks = total_len // LANES
    per_shard = blocks // shards_of
    k = np.arange(blocks)[:, None]
    a = np.arange(blocks)[None, :]
    angle = np.pi * (2 * k + 1) * a / (2 * blocks)
    outer = np.concatenate([np.cos(angle), -np.sin(angle)], axis=0)
    inverse = np.concatenate([np.cos(angle).T, -np.sin(angle).T], axis=1) / total_len
    filter_inverse = inverse / math.sqrt(total_len)
    order = [
        np.concatenate(
            [np.arange(per_shard) + (me ^ d) * per_shard for d in range(shards_of)]
        )
        for me in range(shards_of)
    ]

    def wide(table):
        high, low = halves(table)
        return np.concatenate([high, high, low], axis=1)

    outer_w = np.stack([wide(outer[:, o]) for o in order])
    inverse_w = np.stack([wide(inverse[o]) for o in order])
    filter_w = np.stack([wide(filter_inverse[o]) for o in order])
    b = np.arange(LANES)[None, :]
    turn = np.pi * (2 * k + 1) * b / (2 * total_len)
    twiddle = np.stack([np.cos(turn), np.sin(turn)]).astype(np.float32)
    q = np.arange(LANES)
    inner = 2 * np.pi * (q[:, None] * q[None, :] % LANES) / LANES
    dft = np.block([[np.cos(inner), -np.sin(inner)], [np.sin(inner), np.cos(inner)]])
    dft_high, dft_low = halves(dft)
    return outer_w, inverse_w, filter_w, twiddle, np.concatenate([dft_high, dft_high, dft_low])


def triple(x, axis):
    high = x.astype(BF16)
    low = (x - high.astype(F32)).astype(BF16)
    return jnp.concatenate([high, low, high], axis=axis)


def matmul(a, b):
    return jnp.dot(a, b, preferred_element_type=F32)


def pack_kernel(shards_of, chunks, q, *refs):
    sources, refs = refs[:6], refs[6:]
    outs, (fields, *held) = refs[:shards_of], refs[shards_of:]
    channels, length = sources[0].shape
    chunk_rows = channels // chunks
    last = q == chunks - 1
    if q == 0:
        *held, sems = held
        rows = slice(0, chunk_rows)
        copies = [
            pltpu.make_async_copy(source.at[rows, :] if i < 5 else source, copied, sems.at[i])
            for i, (source, copied) in enumerate(zip(sources, held))
        ]
        for copy in copies:
            copy.start()
        for copy in copies:
            copy.wait()
        sources = held
    post, pre, signal, cotangent, taps, skip_gain = sources
    me = lax.axis_index("seq")
    width = chunk_rows // shards_of
    per = length // LANES
    field_rows = width * per
    turn = lax.broadcasted_iota(jnp.int32, (channels, channels), 0)
    lane = lax.broadcasted_iota(jnp.int32, (channels, channels), 1)
    gains = jnp.broadcast_to(skip_gain[...], (channels, channels))
    gain = jnp.sum(jnp.where(turn == lane, gains, 0.0), axis=1, keepdims=True)
    first = (lax.broadcasted_iota(jnp.int32, (16, LANES), 1) == 0) & (me == 0)
    parts = []
    for c in range(0 if last else q * chunk_rows, (q + 1) * chunk_rows, 16):
        rows = slice(c, c + 16)
        g = pre[rows, :].astype(F32) * signal[rows, :].astype(F32)
        dc = cotangent[rows, :].astype(F32) * post[rows, :].astype(F32)
        if c >= q * chunk_rows:
            to = slice(c - q * chunk_rows, c - q * chunk_rows + 16)
            fields[0, to, :] = taps[rows, :]
            fields[0, to, :LANES] = taps[rows, :LANES] + jnp.where(first, gain[rows], 0.0)
            fields[1, to, :] = g
            fields[2, to, :] = dc
        if last:
            prod = g * dc
            parts.append(sum(prod[:, a * LANES : (a + 1) * LANES] for a in range(per)))
    for d in range(shards_of):
        for f in range(3):
            for c in range(0, width, SUBLANES):
                rows = pl.ds(pl.multiple_of((me ^ d) * width + c, SUBLANES), SUBLANES)
                for a in range(per):
                    outs[d][pl.ds(f * field_rows + c * per + a, SUBLANES, stride=per), :] = fields[
                        f, rows, a * LANES : (a + 1) * LANES
                    ]
    if last:
        folded = jnp.concatenate(parts + [jnp.zeros((LANES - channels, LANES), F32)], axis=0)
        skip = jnp.sum(folded.T, axis=0, keepdims=True)
        for d in range(shards_of):
            outs[d][3 * field_rows :, :] = jnp.broadcast_to(skip, (SUBLANES, LANES))


def spectral_kernel(shards_of, chunks, last, channels, per, *refs):
    outer_w, inverse_w, filter_w, twiddle, dft = refs[:5]
    pieces = refs[5 : 5 + shards_of]
    outs = refs[5 + shards_of : 5 + 2 * shards_of]
    rest = refs[5 + 2 * shards_of :]
    if last:
        d_skip, *rest = rest
    spectra, packed = rest
    me = lax.axis_index("seq")
    chunk_rows = channels // chunks
    width = chunk_rows // shards_of
    blocks = shards_of * per
    field_rows = width * per
    spectrum_rows = width * blocks
    cos_t = twiddle[0]
    sin_t = twiddle[1]
    forward = outer_w[me]
    back = (inverse_w[me], inverse_w[me], filter_w[me])
    if last:
        skips = sum(pieces[d][3 * field_rows : 3 * field_rows + 1, :] for d in range(shards_of))
        d_skip[...] = skips[:, : d_skip.shape[1]] * (1.0 / math.sqrt(blocks * LANES))

    def held(f, ch):
        start = f * field_rows + ch * per
        return jnp.concatenate([pieces[d][start : start + per, :] for d in range(shards_of)], axis=0)

    def spectrum(f, ch):
        start = f * spectrum_rows + ch * blocks
        return slice(start, start + blocks)

    def inner(f):
        rows = slice(f * spectrum_rows, (f + 1) * spectrum_rows)
        spectra[rows, :] = matmul(packed[rows, :], dft[...])

    for f in range(3):
        for c in range(0, width, 2):
            x = jnp.concatenate([held(f, c), held(f, c + 1)], axis=1)
            mixed = matmul(forward, triple(x, 0))
            for i in range(2):
                real = mixed[:blocks, i * LANES : (i + 1) * LANES]
                imag = mixed[blocks:, i * LANES : (i + 1) * LANES]
                turned = [real * cos_t + imag * sin_t, imag * cos_t - real * sin_t]
                packed[spectrum(f, c + i), :] = triple(jnp.concatenate(turned, axis=1), 1)
    for f in range(3):
        inner(f)
    for ch in range(width):
        tr, ti = spectra[spectrum(0, ch), :LANES], spectra[spectrum(0, ch), LANES:]
        gr, gi = spectra[spectrum(1, ch), :LANES], spectra[spectrum(1, ch), LANES:]
        dr, di = spectra[spectrum(2, ch), :LANES], spectra[spectrum(2, ch), LANES:]
        products = (
            (gr * tr - gi * ti, gr * ti + gi * tr),
            (tr * dr + ti * di, tr * di - ti * dr),
            (gr * dr + gi * di, gr * di - gi * dr),
        )
        for f, (real, imag) in enumerate(products):
            packed[spectrum(f, ch), :] = triple(jnp.concatenate([imag, real], axis=1), 1)
    for f in range(3):
        inner(f)
    for f in range(3):
        for c in range(0, width, 2):
            turned = []
            for ch in (c, c + 1):
                imag, real = spectra[spectrum(f, ch), :LANES], spectra[spectrum(f, ch), LANES:]
                both = [real * cos_t - imag * sin_t, imag * cos_t + real * sin_t]
                turned.append(jnp.concatenate(both, axis=0))
            y = matmul(back[f], triple(jnp.concatenate(turned, axis=1), 0))
            for i in range(2):
                start = f * field_rows + (c + i) * per
                for d in range(shards_of):
                    outs[d][start : start + per, :] = y[
                        d * per : (d + 1) * per, i * LANES : (i + 1) * LANES
                    ]


def gate_kernel(shards_of, chunks, *refs):
    post, pre, signal, cotangent = refs[:4]
    pieces = refs[4 : 4 + chunks * shards_of]
    refs = refs[4 + chunks * shards_of :]
    outs, (fields, output, d_post, d_pre, d_signal, sems) = refs[:5], refs[5:]
    me = lax.axis_index("seq")
    channels, length = post.shape
    chunk_rows = channels // chunks
    width = chunk_rows // shards_of
    per = length // LANES
    field_rows = width * per
    copies = []

    def ship(q, i, held):
        rows = pl.ds(q * chunk_rows, chunk_rows)
        copy = pltpu.make_async_copy(held.at[rows, :], outs[i].at[rows, :], sems.at[q, i])
        copy.start()
        copies.append(copy)

    def gather(q, f):
        for d in range(shards_of):
            for c in range(0, width, SUBLANES):
                top = q * chunk_rows + (me ^ d) * width + c
                held = pl.ds(pl.multiple_of(top, SUBLANES), SUBLANES)
                for a in range(per):
                    fields[f, held, a * LANES : (a + 1) * LANES] = pieces[q * shards_of + d][
                        pl.ds(f * field_rows + c * per + a, SUBLANES, stride=per), :
                    ]

    for q in range(chunks):
        rows = slice(q * chunk_rows, (q + 1) * chunk_rows)
        gather(q, 2)
        ship(q, 4, fields.at[2])
        gather(q, 0)
        conved = fields[0, rows, :]
        output[rows, :] = (post[rows, :].astype(F32) * conved).astype(BF16)
        ship(q, 0, output)
        d_post[rows, :] = (cotangent[rows, :].astype(F32) * conved).astype(BF16)
        ship(q, 1, d_post)
        gather(q, 1)
        d_gated = fields[1, rows, :]
        d_pre[rows, :] = (signal[rows, :].astype(F32) * d_gated).astype(BF16)
        ship(q, 2, d_pre)
        d_signal[rows, :] = (pre[rows, :].astype(F32) * d_gated).astype(BF16)
        ship(q, 3, d_signal)
    for copy in copies:
        copy.wait()


def shards(post_gate, pre_gate, signal, cotangent, filter_taps, skip_gain):
    shards_of = lax.axis_size("seq")
    channels, length = post_gate.shape
    chunks = CHUNKS if channels % (CHUNKS * shards_of * SUBLANES) == 0 else 1
    chunk_rows = channels // chunks
    width = chunk_rows // shards_of
    per = length // LANES
    field_rows = width * per
    total_len = shards_of * length
    vmem = pl.BlockSpec(memory_space=pltpu.VMEM)
    hbm = pl.BlockSpec(memory_space=pltpu.HBM)
    params = pltpu.CompilerParams(vmem_limit_bytes=48 * 2**20)

    def swap(pieces):
        moved = {
            d: lax.ppermute(pieces[d], "seq", [(i, i ^ d) for i in range(shards_of)])
            for d in reversed(range(1, shards_of))
        }
        return [pieces[0]] + [moved[d] for d in range(1, shards_of)]

    def rows(count):
        return [jax.ShapeDtypeStruct((count, LANES), F32)] * shards_of

    arrays = (post_gate, pre_gate, signal, cotangent, filter_taps, skip_gain.reshape(1, channels))
    arrived = []
    for q in range(chunks):
        last = q == chunks - 1
        scratch = [pltpu.VMEM((3, chunk_rows, length), F32)]
        if q == 0:
            scratch += [pltpu.VMEM((chunk_rows, length), BF16)] * 4
            scratch += [pltpu.VMEM((chunk_rows, length), F32), pltpu.VMEM((1, channels), F32)]
            scratch += [pltpu.SemaphoreType.DMA((6,))]
        packed = pl.pallas_call(
            functools.partial(pack_kernel, shards_of, chunks, q),
            out_shape=rows(3 * field_rows + SUBLANES * last),
            in_specs=[hbm if q == 0 else vmem] * 6,
            out_specs=[vmem] * shards_of,
            scratch_shapes=scratch,
            compiler_params=params,
        )(*(pltpu.with_memory_space_constraint(x, pltpu.HBM) if q == 0 else x for x in arrays))
        arrived.append(swap(packed))
    consts = [jnp.asarray(t) for t in tables(shards_of, total_len)]
    spectrum_rows = width * shards_of * per
    back = []
    for q in range(chunks):
        last = q == chunks - 1
        mixed = pl.pallas_call(
            functools.partial(spectral_kernel, shards_of, chunks, last, channels, per),
            out_shape=rows(3 * field_rows) + [jax.ShapeDtypeStruct((1, channels), F32)] * last,
            in_specs=[vmem] * (5 + shards_of),
            out_specs=[vmem] * (shards_of + last),
            scratch_shapes=[
                pltpu.VMEM((3 * spectrum_rows, 2 * LANES), F32),
                pltpu.VMEM((3 * spectrum_rows, 6 * LANES), BF16),
            ],
            compiler_params=params,
        )(*consts, *arrived[q])
        if last:
            d_skip = mixed[shards_of]
        back += swap(mixed[:shards_of])
    output, d_post, d_pre, d_signal, d_filter = pl.pallas_call(
        functools.partial(gate_kernel, shards_of, chunks),
        out_shape=[pltpu.HBM((channels, length), BF16)] * 4 + [pltpu.HBM((channels, length), F32)],
        in_specs=[vmem] * (4 + chunks * shards_of),
        out_specs=[hbm] * 5,
        scratch_shapes=[pltpu.VMEM((3, channels, length), F32)]
        + [pltpu.VMEM((channels, length), BF16)] * 4
        + [pltpu.SemaphoreType.DMA((chunks, 5))],
        compiler_params=params,
    )(post_gate, pre_gate, signal, cotangent, *back)
    return (output, d_post, d_pre, d_signal, d_skip.reshape(channels), d_filter)


def solution(mesh):
    both = P("chan", "seq")
    return jax.shard_map(
        shards,
        mesh=mesh,
        in_specs=(both,) * 5 + (P("chan"),),
        out_specs=(both,) * 4 + (P("chan"), both),
        check_vma=False,
    )
```

```python
import functools
import math

import jax
import jax.numpy as jnp
import ml_dtypes
import numpy as np
from jax import lax
from jax.experimental import pallas as pl
from jax.experimental.pallas import tpu as pltpu
from jax.sharding import PartitionSpec as P

LANES = 128
SUBLANES = 8
CHUNKS = 2
BF16 = jnp.bfloat16
F32 = jnp.float32


def halves(table):
    high = table.astype(np.float32).astype(ml_dtypes.bfloat16)
    low = (table - high.astype(np.float64)).astype(np.float32).astype(ml_dtypes.bfloat16)
    return high, low


def tables(shards_of, total_len):
    blocks = total_len // LANES
    per_shard = blocks // shards_of
    k = np.arange(blocks)[:, None]
    a = np.arange(blocks)[None, :]
    angle = np.pi * (2 * k + 1) * a / (2 * blocks)
    outer = np.concatenate([np.cos(angle), -np.sin(angle)], axis=0)
    inverse = np.concatenate([np.cos(angle).T, -np.sin(angle).T], axis=1) / total_len
    filter_inverse = inverse / math.sqrt(total_len)
    order = [
        np.concatenate(
            [np.arange(per_shard) + (me ^ d) * per_shard for d in range(shards_of)]
        )
        for me in range(shards_of)
    ]

    def wide(table):
        high, low = halves(table)
        return np.concatenate([high, high, low], axis=1)

    outer_w = np.stack([wide(outer[:, o]) for o in order])
    inverse_w = np.stack([wide(inverse[o]) for o in order])
    filter_w = np.stack([wide(filter_inverse[o]) for o in order])
    b = np.arange(LANES)[None, :]
    turn = np.pi * (2 * k + 1) * b / (2 * total_len)
    twiddle = np.stack([np.cos(turn), np.sin(turn)]).astype(np.float32)
    q = np.arange(LANES)
    inner = 2 * np.pi * (q[:, None] * q[None, :] % LANES) / LANES
    dft = np.block([[np.cos(inner), -np.sin(inner)], [np.sin(inner), np.cos(inner)]])
    dft_high, dft_low = halves(dft)
    return outer_w, inverse_w, filter_w, twiddle, np.concatenate([dft_high, dft_high, dft_low])


def triple(x, axis):
    high = x.astype(BF16)
    low = (x - high.astype(F32)).astype(BF16)
    return jnp.concatenate([high, low, high], axis=axis)


def matmul(a, b):
    return jnp.dot(a, b, preferred_element_type=F32)


def pack_kernel(shards_of, chunks, q, *refs):
    sources, refs = refs[:6], refs[6:]
    outs, (fields, *held) = refs[:shards_of], refs[shards_of:]
    channels, length = sources[0].shape
    chunk_rows = channels // chunks
    last = q == chunks - 1
    if q == 0:
        *held, sems = held
        rows = slice(0, chunk_rows)
        copies = [
            pltpu.make_async_copy(source.at[rows, :] if i < 5 else source, copied, sems.at[i])
            for i, (source, copied) in enumerate(zip(sources, held))
        ]
        for copy in copies:
            copy.start()
        for copy in copies:
            copy.wait()
        sources = held
    post, pre, signal, cotangent, taps, skip_gain = sources
    me = lax.axis_index("seq")
    width = chunk_rows // shards_of
    per = length // LANES
    field_rows = width * per
    turn = lax.broadcasted_iota(jnp.int32, (channels, channels), 0)
    lane = lax.broadcasted_iota(jnp.int32, (channels, channels), 1)
    gains = jnp.broadcast_to(skip_gain[...], (channels, channels))
    gain = jnp.sum(jnp.where(turn == lane, gains, 0.0), axis=1, keepdims=True)
    first = (lax.broadcasted_iota(jnp.int32, (16, LANES), 1) == 0) & (me == 0)
    parts = []
    for c in range(0 if last else q * chunk_rows, (q + 1) * chunk_rows, 16):
        rows = slice(c, c + 16)
        g = pre[rows, :].astype(F32) * signal[rows, :].astype(F32)
        dc = cotangent[rows, :].astype(F32) * post[rows, :].astype(F32)
        if c >= q * chunk_rows:
            to = slice(c - q * chunk_rows, c - q * chunk_rows + 16)
            fields[0, to, :] = taps[rows, :]
            fields[0, to, :LANES] = taps[rows, :LANES] + jnp.where(first, gain[rows], 0.0)
            fields[1, to, :] = g
            fields[2, to, :] = dc
        if last:
            prod = g * dc
            parts.append(sum(prod[:, a * LANES : (a + 1) * LANES] for a in range(per)))
    for d in range(shards_of):
        for f in range(3):
            for c in range(0, width, SUBLANES):
                rows = pl.ds(pl.multiple_of((me ^ d) * width + c, SUBLANES), SUBLANES)
                for a in range(per):
                    outs[d][pl.ds(f * field_rows + c * per + a, SUBLANES, stride=per), :] = fields[
                        f, rows, a * LANES : (a + 1) * LANES
                    ]
    if last:
        folded = jnp.concatenate(parts + [jnp.zeros((LANES - channels, LANES), F32)], axis=0)
        skip = jnp.sum(folded.T, axis=0, keepdims=True)
        for d in range(shards_of):
            outs[d][3 * field_rows :, :] = jnp.broadcast_to(skip, (SUBLANES, LANES))


def spectral_kernel(shards_of, chunks, last, channels, per, *refs):
    outer_w, inverse_w, filter_w, twiddle, dft = refs[:5]
    pieces = refs[5 : 5 + shards_of]
    outs = refs[5 + shards_of : 5 + 2 * shards_of]
    rest = refs[5 + 2 * shards_of :]
    if last:
        d_skip, *rest = rest
    spectra, packed = rest
    me = lax.axis_index("seq")
    chunk_rows = channels // chunks
    width = chunk_rows // shards_of
    blocks = shards_of * per
    field_rows = width * per
    spectrum_rows = width * blocks
    cos_t = twiddle[0]
    sin_t = twiddle[1]
    forward = outer_w[me]
    back = (inverse_w[me], inverse_w[me], filter_w[me])
    if last:
        skips = sum(pieces[d][3 * field_rows : 3 * field_rows + 1, :] for d in range(shards_of))
        d_skip[...] = skips[:, : d_skip.shape[1]] * (1.0 / math.sqrt(blocks * LANES))

    def held(f, ch):
        start = f * field_rows + ch * per
        return jnp.concatenate([pieces[d][start : start + per, :] for d in range(shards_of)], axis=0)

    def spectrum(f, ch):
        start = f * spectrum_rows + ch * blocks
        return slice(start, start + blocks)

    def inner(f):
        rows = slice(f * spectrum_rows, (f + 1) * spectrum_rows)
        spectra[rows, :] = matmul(packed[rows, :], dft[...])

    for f in range(3):
        for c in range(0, width, 2):
            x = jnp.concatenate([held(f, c), held(f, c + 1)], axis=1)
            mixed = matmul(forward, triple(x, 0))
            for i in range(2):
                real = mixed[:blocks, i * LANES : (i + 1) * LANES]
                imag = mixed[blocks:, i * LANES : (i + 1) * LANES]
                turned = [real * cos_t + imag * sin_t, imag * cos_t - real * sin_t]
                packed[spectrum(f, c + i), :] = triple(jnp.concatenate(turned, axis=1), 1)
    for f in range(3):
        inner(f)
    for ch in range(width):
        tr, ti = spectra[spectrum(0, ch), :LANES], spectra[spectrum(0, ch), LANES:]
        gr, gi = spectra[spectrum(1, ch), :LANES], spectra[spectrum(1, ch), LANES:]
        dr, di = spectra[spectrum(2, ch), :LANES], spectra[spectrum(2, ch), LANES:]
        products = (
            (gr * tr - gi * ti, gr * ti + gi * tr),
            (tr * dr + ti * di, tr * di - ti * dr),
            (gr * dr + gi * di, gr * di - gi * dr),
        )
        for f, (real, imag) in enumerate(products):
            packed[spectrum(f, ch), :] = triple(jnp.concatenate([imag, real], axis=1), 1)
    for f in range(3):
        inner(f)
    for f in range(3):
        for c in range(0, width, 2):
            turned = []
            for ch in (c, c + 1):
                imag, real = spectra[spectrum(f, ch), :LANES], spectra[spectrum(f, ch), LANES:]
                both = [real * cos_t - imag * sin_t, imag * cos_t + real * sin_t]
                turned.append(jnp.concatenate(both, axis=0))
            y = matmul(back[f], triple(jnp.concatenate(turned, axis=1), 0))
            for i in range(2):
                start = f * field_rows + (c + i) * per
                for d in range(shards_of):
                    outs[d][start : start + per, :] = y[
                        d * per : (d + 1) * per, i * LANES : (i + 1) * LANES
                    ]


def gate_kernel(shards_of, chunks, *refs):
    post, pre, signal, cotangent, skip = refs[:5]
    pieces = refs[5 : 5 + chunks * shards_of]
    refs = refs[5 + chunks * shards_of :]
    outs, (fields, output, d_post, d_pre, d_signal, sems) = refs[:6], refs[6:]
    me = lax.axis_index("seq")
    channels, length = post.shape
    chunk_rows = channels // chunks
    width = chunk_rows // shards_of
    per = length // LANES
    field_rows = width * per
    copies = [pltpu.make_async_copy(skip, outs[5], sems.at[0, 5])]
    copies[0].start()

    def ship(q, i, held):
        rows = pl.ds(q * chunk_rows, chunk_rows)
        copy = pltpu.make_async_copy(held.at[rows, :], outs[i].at[rows, :], sems.at[q, i])
        copy.start()
        copies.append(copy)

    def gather(q, f):
        for d in range(shards_of):
            for c in range(0, width, SUBLANES):
                top = q * chunk_rows + (me ^ d) * width + c
                held = pl.ds(pl.multiple_of(top, SUBLANES), SUBLANES)
                for a in range(per):
                    fields[f, held, a * LANES : (a + 1) * LANES] = pieces[q * shards_of + d][
                        pl.ds(f * field_rows + c * per + a, SUBLANES, stride=per), :
                    ]

    for q in range(chunks):
        rows = slice(q * chunk_rows, (q + 1) * chunk_rows)
        gather(q, 2)
        ship(q, 4, fields.at[2])
        gather(q, 0)
        conved = fields[0, rows, :]
        output[rows, :] = (post[rows, :].astype(F32) * conved).astype(BF16)
        ship(q, 0, output)
        d_post[rows, :] = (cotangent[rows, :].astype(F32) * conved).astype(BF16)
        ship(q, 1, d_post)
        gather(q, 1)
        d_gated = fields[1, rows, :]
        d_pre[rows, :] = (signal[rows, :].astype(F32) * d_gated).astype(BF16)
        ship(q, 2, d_pre)
        d_signal[rows, :] = (pre[rows, :].astype(F32) * d_gated).astype(BF16)
        ship(q, 3, d_signal)
    for copy in copies:
        copy.wait()


def shards(post_gate, pre_gate, signal, cotangent, filter_taps, skip_gain):
    shards_of = lax.axis_size("seq")
    channels, length = post_gate.shape
    chunks = CHUNKS if channels % (CHUNKS * shards_of * SUBLANES) == 0 else 1
    chunk_rows = channels // chunks
    width = chunk_rows // shards_of
    per = length // LANES
    field_rows = width * per
    total_len = shards_of * length
    vmem = pl.BlockSpec(memory_space=pltpu.VMEM)
    hbm = pl.BlockSpec(memory_space=pltpu.HBM)
    params = pltpu.CompilerParams(vmem_limit_bytes=48 * 2**20)

    def swap(pieces):
        moved = {
            d: lax.ppermute(pieces[d], "seq", [(i, i ^ d) for i in range(shards_of)])
            for d in reversed(range(1, shards_of))
        }
        return [pieces[0]] + [moved[d] for d in range(1, shards_of)]

    def rows(count):
        return [jax.ShapeDtypeStruct((count, LANES), F32)] * shards_of

    arrays = (post_gate, pre_gate, signal, cotangent, filter_taps, skip_gain.reshape(1, channels))
    arrived = []
    for q in range(chunks):
        last = q == chunks - 1
        scratch = [pltpu.VMEM((3, chunk_rows, length), F32)]
        if q == 0:
            scratch += [pltpu.VMEM((chunk_rows, length), BF16)] * 4
            scratch += [pltpu.VMEM((chunk_rows, length), F32), pltpu.VMEM((1, channels), F32)]
            scratch += [pltpu.SemaphoreType.DMA((6,))]
        packed = pl.pallas_call(
            functools.partial(pack_kernel, shards_of, chunks, q),
            out_shape=rows(3 * field_rows + SUBLANES * last),
            in_specs=[hbm if q == 0 else vmem] * 6,
            out_specs=[vmem] * shards_of,
            scratch_shapes=scratch,
            compiler_params=params,
        )(*(pltpu.with_memory_space_constraint(x, pltpu.HBM) if q == 0 else x for x in arrays))
        arrived.append(swap(packed))
    consts = [jnp.asarray(t) for t in tables(shards_of, total_len)]
    spectrum_rows = width * shards_of * per
    back = []
    for q in range(chunks):
        last = q == chunks - 1
        mixed = pl.pallas_call(
            functools.partial(spectral_kernel, shards_of, chunks, last, channels, per),
            out_shape=rows(3 * field_rows) + [jax.ShapeDtypeStruct((1, channels), F32)] * last,
            in_specs=[vmem] * (5 + shards_of),
            out_specs=[vmem] * (shards_of + last),
            scratch_shapes=[
                pltpu.VMEM((3 * spectrum_rows, 2 * LANES), F32),
                pltpu.VMEM((3 * spectrum_rows, 6 * LANES), BF16),
            ],
            compiler_params=params,
        )(*consts, *arrived[q])
        if last:
            d_skip = mixed[shards_of]
        back += swap(mixed[:shards_of])
    output, d_post, d_pre, d_signal, d_filter, d_skip = pl.pallas_call(
        functools.partial(gate_kernel, shards_of, chunks),
        out_shape=[pltpu.HBM((channels, length), BF16)] * 4
        + [pltpu.HBM((channels, length), F32), pltpu.HBM((1, channels), F32)],
        in_specs=[vmem] * (5 + chunks * shards_of),
        out_specs=[hbm] * 6,
        scratch_shapes=[pltpu.VMEM((3, channels, length), F32)]
        + [pltpu.VMEM((channels, length), BF16)] * 4
        + [pltpu.SemaphoreType.DMA((chunks, 6))],
        compiler_params=params,
    )(post_gate, pre_gate, signal, cotangent, d_skip, *back)
    return (output, d_post, d_pre, d_signal, d_skip.reshape(channels), d_filter)


def solution(mesh):
    both = P("chan", "seq")
    return jax.shard_map(
        shards,
        mesh=mesh,
        in_specs=(both,) * 5 + (P("chan"),),
        out_specs=(both,) * 4 + (P("chan"), both),
        check_vma=False,
    )
```

```python
import functools
import math

import jax
import jax.numpy as jnp
import ml_dtypes
import numpy as np
from jax import lax
from jax.experimental import pallas as pl
from jax.experimental.pallas import tpu as pltpu
from jax.sharding import PartitionSpec as P

LANES = 128
SUBLANES = 8
CHUNKS = 2
BF16 = jnp.bfloat16
F32 = jnp.float32


def halves(table):
    high = table.astype(np.float32).astype(ml_dtypes.bfloat16)
    low = (table - high.astype(np.float64)).astype(np.float32).astype(ml_dtypes.bfloat16)
    return high, low


def tables(shards_of, total_len):
    blocks = total_len // LANES
    per_shard = blocks // shards_of
    k = np.arange(blocks)[:, None]
    a = np.arange(blocks)[None, :]
    angle = np.pi * (2 * k + 1) * a / (2 * blocks)
    outer = np.concatenate([np.cos(angle), -np.sin(angle)], axis=0)
    inverse = np.concatenate([np.cos(angle).T, -np.sin(angle).T], axis=1) / total_len
    filter_inverse = inverse / math.sqrt(total_len)
    order = [
        np.concatenate(
            [np.arange(per_shard) + (me ^ d) * per_shard for d in range(shards_of)]
        )
        for me in range(shards_of)
    ]

    def wide(table):
        high, low = halves(table)
        return np.concatenate([high, high, low], axis=1)

    outer_w = np.stack([wide(outer[:, o]) for o in order])
    inverse_w = np.stack([wide(inverse[o]) for o in order])
    filter_w = np.stack([wide(filter_inverse[o]) for o in order])
    b = np.arange(LANES)[None, :]
    turn = np.pi * (2 * k + 1) * b / (2 * total_len)
    twiddle = np.stack([np.cos(turn), np.sin(turn)]).astype(np.float32)
    q = np.arange(LANES)
    inner = 2 * np.pi * (q[:, None] * q[None, :] % LANES) / LANES
    dft = np.block([[np.cos(inner), -np.sin(inner)], [np.sin(inner), np.cos(inner)]])
    dft_high, dft_low = halves(dft)
    return outer_w, inverse_w, filter_w, twiddle, np.concatenate([dft_high, dft_high, dft_low])


def triple(x, axis):
    high = x.astype(BF16)
    low = (x - high.astype(F32)).astype(BF16)
    return jnp.concatenate([high, low, high], axis=axis)


def matmul(a, b):
    return jnp.dot(a, b, preferred_element_type=F32)


def pack_kernel(shards_of, chunks, q, *refs):
    sources, refs = refs[:6], refs[6:]
    outs, (fields, *held) = refs[:shards_of], refs[shards_of:]
    channels, length = sources[0].shape
    chunk_rows = channels // chunks
    last = q == chunks - 1
    if q == 0:
        *held, sems = held
        rows = slice(0, chunk_rows)
        copies = [
            pltpu.make_async_copy(source.at[rows, :] if i < 5 else source, copied, sems.at[i])
            for i, (source, copied) in enumerate(zip(sources, held))
        ]
        for copy in copies:
            copy.start()
        for copy in copies:
            copy.wait()
        sources = held
    post, pre, signal, cotangent, taps, skip_gain = sources
    me = lax.axis_index("seq")
    width = chunk_rows // shards_of
    per = length // LANES
    field_rows = width * per
    turn = lax.broadcasted_iota(jnp.int32, (channels, channels), 0)
    lane = lax.broadcasted_iota(jnp.int32, (channels, channels), 1)
    gains = jnp.broadcast_to(skip_gain[...], (channels, channels))
    gain = jnp.sum(jnp.where(turn == lane, gains, 0.0), axis=1, keepdims=True)
    first = (lax.broadcasted_iota(jnp.int32, (16, LANES), 1) == 0) & (me == 0)
    parts = []
    for c in range(0 if last else q * chunk_rows, (q + 1) * chunk_rows, 16):
        rows = slice(c, c + 16)
        g = pre[rows, :].astype(F32) * signal[rows, :].astype(F32)
        dc = cotangent[rows, :].astype(F32) * post[rows, :].astype(F32)
        if c >= q * chunk_rows:
            to = slice(c - q * chunk_rows, c - q * chunk_rows + 16)
            fields[0, to, :] = taps[rows, :]
            fields[0, to, :LANES] = taps[rows, :LANES] + jnp.where(first, gain[rows], 0.0)
            fields[1, to, :] = g
            fields[2, to, :] = dc
        if last:
            prod = g * dc
            parts.append(sum(prod[:, a * LANES : (a + 1) * LANES] for a in range(per)))
    for d in range(shards_of):
        for f in range(3):
            for c in range(0, width, SUBLANES):
                rows = pl.ds(pl.multiple_of((me ^ d) * width + c, SUBLANES), SUBLANES)
                for a in range(per):
                    outs[d][pl.ds(f * field_rows + c * per + a, SUBLANES, stride=per), :] = fields[
                        f, rows, a * LANES : (a + 1) * LANES
                    ]
    if last:
        folded = jnp.concatenate(parts + [jnp.zeros((LANES - channels, LANES), F32)], axis=0)
        skip = jnp.sum(folded.T, axis=0, keepdims=True)
        for d in range(shards_of):
            outs[d][3 * field_rows :, :] = jnp.broadcast_to(skip, (SUBLANES, LANES))


def spectral_kernel(shards_of, chunks, last, channels, per, *refs):
    outer_w, inverse_w, filter_w, twiddle, dft = refs[:5]
    pieces = refs[5 : 5 + shards_of]
    outs = refs[5 + shards_of : 5 + 2 * shards_of]
    rest = refs[5 + 2 * shards_of :]
    if last:
        d_skip, *rest = rest
    spectra, packed = rest
    me = lax.axis_index("seq")
    chunk_rows = channels // chunks
    width = chunk_rows // shards_of
    blocks = shards_of * per
    field_rows = width * per
    spectrum_rows = width * blocks
    cos_t = twiddle[0]
    sin_t = twiddle[1]
    forward = outer_w[me]
    back = (inverse_w[me], inverse_w[me], filter_w[me])
    if last:
        skips = sum(pieces[d][3 * field_rows : 3 * field_rows + 1, :] for d in range(shards_of))
        d_skip[...] = skips[:, : d_skip.shape[1]] * (1.0 / math.sqrt(blocks * LANES))

    def held(f, ch):
        start = f * field_rows + ch * per
        return jnp.concatenate([pieces[d][start : start + per, :] for d in range(shards_of)], axis=0)

    def spectrum(f, ch):
        start = f * spectrum_rows + ch * blocks
        return slice(start, start + blocks)

    def inner(f):
        rows = slice(f * spectrum_rows, (f + 1) * spectrum_rows)
        spectra[rows, :] = matmul(packed[rows, :], dft[...])

    for f in range(3):
        for c in range(0, width, 2):
            x = jnp.concatenate([held(f, c), held(f, c + 1)], axis=1)
            mixed = matmul(forward, triple(x, 0))
            for i in range(2):
                real = mixed[:blocks, i * LANES : (i + 1) * LANES]
                imag = mixed[blocks:, i * LANES : (i + 1) * LANES]
                turned = [real * cos_t + imag * sin_t, imag * cos_t - real * sin_t]
                packed[spectrum(f, c + i), :] = triple(jnp.concatenate(turned, axis=1), 1)
    for f in range(3):
        inner(f)
    for ch in range(width):
        tr, ti = spectra[spectrum(0, ch), :LANES], spectra[spectrum(0, ch), LANES:]
        gr, gi = spectra[spectrum(1, ch), :LANES], spectra[spectrum(1, ch), LANES:]
        dr, di = spectra[spectrum(2, ch), :LANES], spectra[spectrum(2, ch), LANES:]
        products = (
            (gr * tr - gi * ti, gr * ti + gi * tr),
            (tr * dr + ti * di, tr * di - ti * dr),
            (gr * dr + gi * di, gr * di - gi * dr),
        )
        for f, (real, imag) in enumerate(products):
            packed[spectrum(f, ch), :] = triple(jnp.concatenate([imag, real], axis=1), 1)
    for f in range(3):
        inner(f)
    for f in range(3):
        for c in range(0, width, 2):
            turned = []
            for ch in (c, c + 1):
                imag, real = spectra[spectrum(f, ch), :LANES], spectra[spectrum(f, ch), LANES:]
                both = [real * cos_t - imag * sin_t, imag * cos_t + real * sin_t]
                turned.append(jnp.concatenate(both, axis=0))
            y = matmul(back[f], triple(jnp.concatenate(turned, axis=1), 0))
            for i in range(2):
                start = f * field_rows + (c + i) * per
                for d in range(shards_of):
                    outs[d][start : start + per, :] = y[
                        d * per : (d + 1) * per, i * LANES : (i + 1) * LANES
                    ]


def gate_kernel(shards_of, chunks, q, *refs):
    post, pre, signal, cotangent = refs[:4]
    pieces = refs[4 : 4 + shards_of]
    last = q == chunks - 1
    refs = refs[4 + shards_of :]
    if last:
        skip, *refs = refs
    else:
        refs = refs[1:]
    refs = refs[5 * (q > 0) :]
    outs, refs = refs[: 5 + last], refs[5 + last :]
    fields, output, d_post, d_pre, d_signal, sems = refs
    me = lax.axis_index("seq")
    channels, length = post.shape
    chunk_rows = channels // chunks
    width = chunk_rows // shards_of
    per = length // LANES
    field_rows = width * per
    rows = slice(q * chunk_rows, (q + 1) * chunk_rows)
    copies = []

    def ship(i, held, target):
        copies.append(pltpu.make_async_copy(held, target, sems.at[i]))
        copies[-1].start()

    def part(i):
        return outs[i].at[pl.ds(q * chunk_rows, chunk_rows), :]

    def gather(f):
        for d in range(shards_of):
            for c in range(0, width, SUBLANES):
                held = pl.ds(pl.multiple_of((me ^ d) * width + c, SUBLANES), SUBLANES)
                for a in range(per):
                    fields[f, held, a * LANES : (a + 1) * LANES] = pieces[d][
                        pl.ds(f * field_rows + c * per + a, SUBLANES, stride=per), :
                    ]

    if last:
        ship(5, skip, outs[5])
    gather(2)
    ship(4, fields.at[2], part(4))
    gather(0)
    conved = fields[0]
    output[...] = (post[rows, :].astype(F32) * conved).astype(BF16)
    ship(0, output, part(0))
    d_post[...] = (cotangent[rows, :].astype(F32) * conved).astype(BF16)
    ship(1, d_post, part(1))
    gather(1)
    d_gated = fields[1]
    d_pre[...] = (signal[rows, :].astype(F32) * d_gated).astype(BF16)
    ship(2, d_pre, part(2))
    d_signal[...] = (pre[rows, :].astype(F32) * d_gated).astype(BF16)
    ship(3, d_signal, part(3))
    for copy in copies:
        copy.wait()


def shards(post_gate, pre_gate, signal, cotangent, filter_taps, skip_gain):
    shards_of = lax.axis_size("seq")
    channels, length = post_gate.shape
    chunks = CHUNKS if channels % (CHUNKS * shards_of * SUBLANES) == 0 else 1
    chunk_rows = channels // chunks
    width = chunk_rows // shards_of
    per = length // LANES
    field_rows = width * per
    total_len = shards_of * length
    vmem = pl.BlockSpec(memory_space=pltpu.VMEM)
    hbm = pl.BlockSpec(memory_space=pltpu.HBM)
    params = pltpu.CompilerParams(vmem_limit_bytes=48 * 2**20)

    def swap(pieces):
        moved = {
            d: lax.ppermute(pieces[d], "seq", [(i, i ^ d) for i in range(shards_of)])
            for d in reversed(range(1, shards_of))
        }
        return [pieces[0]] + [moved[d] for d in range(1, shards_of)]

    def rows(count):
        return [jax.ShapeDtypeStruct((count, LANES), F32)] * shards_of

    arrays = (post_gate, pre_gate, signal, cotangent, filter_taps, skip_gain.reshape(1, channels))
    arrived = []
    for q in range(chunks):
        last = q == chunks - 1
        scratch = [pltpu.VMEM((3, chunk_rows, length), F32)]
        if q == 0:
            scratch += [pltpu.VMEM((chunk_rows, length), BF16)] * 4
            scratch += [pltpu.VMEM((chunk_rows, length), F32), pltpu.VMEM((1, channels), F32)]
            scratch += [pltpu.SemaphoreType.DMA((6,))]
        packed = pl.pallas_call(
            functools.partial(pack_kernel, shards_of, chunks, q),
            out_shape=rows(3 * field_rows + SUBLANES * last),
            in_specs=[hbm if q == 0 else vmem] * 6,
            out_specs=[vmem] * shards_of,
            scratch_shapes=scratch,
            compiler_params=params,
        )(*(pltpu.with_memory_space_constraint(x, pltpu.HBM) if q == 0 else x for x in arrays))
        arrived.append(swap(packed))
    consts = [jnp.asarray(t) for t in tables(shards_of, total_len)]
    spectrum_rows = width * shards_of * per
    back = []
    for q in range(chunks):
        last = q == chunks - 1
        mixed = pl.pallas_call(
            functools.partial(spectral_kernel, shards_of, chunks, last, channels, per),
            out_shape=rows(3 * field_rows) + [jax.ShapeDtypeStruct((1, channels), F32)] * last,
            in_specs=[vmem] * (5 + shards_of),
            out_specs=[vmem] * (shards_of + last),
            scratch_shapes=[
                pltpu.VMEM((3 * spectrum_rows, 2 * LANES), F32),
                pltpu.VMEM((3 * spectrum_rows, 6 * LANES), BF16),
            ],
            compiler_params=params,
        )(*consts, *arrived[q])
        if last:
            d_skip = mixed[shards_of]
        back.append(swap(mixed[:shards_of]))
    outs = []
    for q in range(chunks):
        last = q == chunks - 1
        outs = pl.pallas_call(
            functools.partial(gate_kernel, shards_of, chunks, q),
            out_shape=[pltpu.HBM((channels, length), BF16)] * 4
            + [pltpu.HBM((channels, length), F32)]
            + [pltpu.HBM((1, channels), F32)] * last,
            in_specs=[vmem] * (5 + shards_of) + [hbm] * len(outs),
            out_specs=[hbm] * (5 + last),
            scratch_shapes=[pltpu.VMEM((3, chunk_rows, length), F32)]
            + [pltpu.VMEM((chunk_rows, length), BF16)] * 4
            + [pltpu.SemaphoreType.DMA((6,))],
            input_output_aliases={5 + shards_of + i: i for i in range(len(outs))},
            compiler_params=params,
        )(
            post_gate,
            pre_gate,
            signal,
            cotangent,
            *back[q],
            d_skip if last else back[q + 1][1],
            *outs,
        )
    output, d_post, d_pre, d_signal, d_filter, d_skip = outs
    return (output, d_post, d_pre, d_signal, d_skip.reshape(channels), d_filter)


def solution(mesh):
    both = P("chan", "seq")
    return jax.shard_map(
        shards,
        mesh=mesh,
        in_specs=(both,) * 5 + (P("chan"),),
        out_specs=(both,) * 4 + (P("chan"), both),
        check_vma=False,
    )
```

```python
import functools
import math

import jax
import jax.numpy as jnp
import ml_dtypes
import numpy as np
from jax import lax
from jax.experimental import pallas as pl
from jax.experimental.pallas import tpu as pltpu
from jax.sharding import PartitionSpec as P

LANES = 128
SUBLANES = 8
CHUNKS = 2
BF16 = jnp.bfloat16
F32 = jnp.float32


def halves(table):
    high = table.astype(np.float32).astype(ml_dtypes.bfloat16)
    low = (table - high.astype(np.float64)).astype(np.float32).astype(ml_dtypes.bfloat16)
    return high, low


def tables(shards_of, total_len):
    blocks = total_len // LANES
    per_shard = blocks // shards_of
    k = np.arange(blocks)[:, None]
    a = np.arange(blocks)[None, :]
    angle = np.pi * (2 * k + 1) * a / (2 * blocks)
    outer = np.concatenate([np.cos(angle), -np.sin(angle)], axis=0)
    inverse = np.concatenate([np.cos(angle).T, -np.sin(angle).T], axis=1) / total_len
    filter_inverse = inverse / math.sqrt(total_len)
    order = [
        np.concatenate(
            [np.arange(per_shard) + (me ^ d) * per_shard for d in range(shards_of)]
        )
        for me in range(shards_of)
    ]

    def wide(table):
        high, low = halves(table)
        return np.concatenate([high, high, low], axis=1)

    outer_w = np.stack([wide(outer[:, o]) for o in order])
    inverse_w = np.stack([wide(inverse[o]) for o in order])
    filter_w = np.stack([wide(filter_inverse[o]) for o in order])
    b = np.arange(LANES)[None, :]
    turn = np.pi * (2 * k + 1) * b / (2 * total_len)
    twiddle = np.stack([np.cos(turn), np.sin(turn)]).astype(np.float32)
    q = np.arange(LANES)
    inner = 2 * np.pi * (q[:, None] * q[None, :] % LANES) / LANES
    dft = np.block([[np.cos(inner), -np.sin(inner)], [np.sin(inner), np.cos(inner)]])
    dft_high, dft_low = halves(dft)
    return outer_w, inverse_w, filter_w, twiddle, np.concatenate([dft_high, dft_low], axis=1)


def triple(x, axis):
    high = x.astype(BF16)
    low = (x - high.astype(F32)).astype(BF16)
    return jnp.concatenate([high, low, high] if axis == 0 else [high, low], axis=axis)


def matmul(a, b):
    return jnp.dot(a, b, preferred_element_type=F32)


def pack_kernel(shards_of, chunks, q, *refs):
    sources, refs = refs[:6], refs[6:]
    outs, (fields, *held) = refs[:shards_of], refs[shards_of:]
    channels, length = sources[0].shape
    chunk_rows = channels // chunks
    last = q == chunks - 1
    if q == 0:
        *held, sems = held
        rows = slice(0, chunk_rows)
        copies = [
            pltpu.make_async_copy(source.at[rows, :] if i < 5 else source, copied, sems.at[i])
            for i, (source, copied) in enumerate(zip(sources, held))
        ]
        for i, copy in enumerate(copies):
            copy.start(priority=i % 2)
        for copy in copies:
            copy.wait()
        sources = held
    post, pre, signal, cotangent, taps, skip_gain = sources
    me = lax.axis_index("seq")
    width = chunk_rows // shards_of
    per = length // LANES
    field_rows = width * per
    turn = lax.broadcasted_iota(jnp.int32, (channels, channels), 0)
    lane = lax.broadcasted_iota(jnp.int32, (channels, channels), 1)
    gains = jnp.broadcast_to(skip_gain[...], (channels, channels))
    gain = jnp.sum(jnp.where(turn == lane, gains, 0.0), axis=1, keepdims=True)
    first = (lax.broadcasted_iota(jnp.int32, (16, LANES), 1) == 0) & (me == 0)
    parts = []
    for c in range(0 if last else q * chunk_rows, (q + 1) * chunk_rows, 16):
        rows = slice(c, c + 16)
        g = pre[rows, :].astype(F32) * signal[rows, :].astype(F32)
        dc = cotangent[rows, :].astype(F32) * post[rows, :].astype(F32)
        if c >= q * chunk_rows:
            to = slice(c - q * chunk_rows, c - q * chunk_rows + 16)
            fields[0, to, :] = taps[rows, :]
            fields[0, to, :LANES] = taps[rows, :LANES] + jnp.where(first, gain[rows], 0.0)
            fields[1, to, :] = g
            fields[2, to, :] = dc
        if last:
            prod = g * dc
            parts.append(sum(prod[:, a * LANES : (a + 1) * LANES] for a in range(per)))
    for d in range(shards_of):
        for f in range(3):
            for c in range(0, width, SUBLANES):
                rows = pl.ds(pl.multiple_of((me ^ d) * width + c, SUBLANES), SUBLANES)
                for a in range(per):
                    outs[d][pl.ds(f * field_rows + c * per + a, SUBLANES, stride=per), :] = fields[
                        f, rows, a * LANES : (a + 1) * LANES
                    ]
    if last:
        folded = jnp.concatenate(parts + [jnp.zeros((LANES - channels, LANES), F32)], axis=0)
        skip = jnp.sum(folded.T, axis=0, keepdims=True)
        for d in range(shards_of):
            outs[d][3 * field_rows :, :] = jnp.broadcast_to(skip, (SUBLANES, LANES))


def spectral_kernel(shards_of, chunks, last, channels, per, *refs):
    outer_w, inverse_w, filter_w, twiddle, dft = refs[:5]
    pieces = refs[5 : 5 + shards_of]
    outs = refs[5 + shards_of : 5 + 2 * shards_of]
    rest = refs[5 + 2 * shards_of :]
    if last:
        d_skip, *rest = rest
    spectra, packed = rest
    me = lax.axis_index("seq")
    chunk_rows = channels // chunks
    width = chunk_rows // shards_of
    blocks = shards_of * per
    field_rows = width * per
    spectrum_rows = width * blocks
    cos_t = twiddle[0]
    sin_t = twiddle[1]
    forward = outer_w[me]
    back = (inverse_w[me], inverse_w[me], filter_w[me])
    if last:
        skips = sum(pieces[d][3 * field_rows : 3 * field_rows + 1, :] for d in range(shards_of))
        d_skip[...] = skips[:, : d_skip.shape[1]] * (1.0 / math.sqrt(blocks * LANES))

    def held(f, ch):
        start = f * field_rows + ch * per
        return jnp.concatenate([pieces[d][start : start + per, :] for d in range(shards_of)], axis=0)

    def spectrum(f, ch):
        start = f * spectrum_rows + ch * blocks
        return slice(start, start + blocks)

    def inner(f):
        rows = slice(f * spectrum_rows, (f + 1) * spectrum_rows)
        x = packed[rows, :]
        wide = matmul(x[:, : 2 * LANES], dft[...])
        spectra[rows, :] = (
            wide[:, : 2 * LANES]
            + wide[:, 2 * LANES :]
            + matmul(x[:, 2 * LANES :], dft[:, : 2 * LANES])
        )

    for f in range(3):
        for c in range(0, width, 2):
            x = jnp.concatenate([held(f, c), held(f, c + 1)], axis=1)
            mixed = matmul(forward, triple(x, 0))
            for i in range(2):
                real = mixed[:blocks, i * LANES : (i + 1) * LANES]
                imag = mixed[blocks:, i * LANES : (i + 1) * LANES]
                turned = [real * cos_t + imag * sin_t, imag * cos_t - real * sin_t]
                packed[spectrum(f, c + i), :] = triple(jnp.concatenate(turned, axis=1), 1)
    for f in range(3):
        inner(f)
    for ch in range(width):
        tr, ti = spectra[spectrum(0, ch), :LANES], spectra[spectrum(0, ch), LANES:]
        gr, gi = spectra[spectrum(1, ch), :LANES], spectra[spectrum(1, ch), LANES:]
        dr, di = spectra[spectrum(2, ch), :LANES], spectra[spectrum(2, ch), LANES:]
        products = (
            (gr * tr - gi * ti, gr * ti + gi * tr),
            (tr * dr + ti * di, tr * di - ti * dr),
            (gr * dr + gi * di, gr * di - gi * dr),
        )
        for f, (real, imag) in enumerate(products):
            packed[spectrum(f, ch), :] = triple(jnp.concatenate([imag, real], axis=1), 1)
    for f in range(3):
        inner(f)
    for f in range(3):
        for c in range(0, width, 2):
            turned = []
            for ch in (c, c + 1):
                imag, real = spectra[spectrum(f, ch), :LANES], spectra[spectrum(f, ch), LANES:]
                both = [real * cos_t - imag * sin_t, imag * cos_t + real * sin_t]
                turned.append(jnp.concatenate(both, axis=0))
            y = matmul(back[f], triple(jnp.concatenate(turned, axis=1), 0))
            for i in range(2):
                start = f * field_rows + (c + i) * per
                for d in range(shards_of):
                    outs[d][start : start + per, :] = y[
                        d * per : (d + 1) * per, i * LANES : (i + 1) * LANES
                    ]


def gate_kernel(shards_of, chunks, work, first, *refs):
    post, pre, signal, cotangent, skip = refs[:5]
    refs = refs[5:]
    pieces = []
    for _, distances in work:
        pieces.append(refs[: len(distances)])
        refs = refs[len(distances) :]
    refs = refs[0 if first else 5 :]
    outs, refs = refs[: 5 + first], refs[5 + first :]
    *held, sems = refs
    me = lax.axis_index("seq")
    channels, length = post.shape
    chunk_rows = channels // chunks
    width = chunk_rows // shards_of
    per = length // LANES
    field_rows = width * per
    copies = []
    if first:
        copies.append(pltpu.make_async_copy(skip, outs[5], sems.at[0, 5]))
        copies[0].start()
    for item, (q, distances) in enumerate(work):
        fields, output, d_post, d_pre, d_signal = held[5 * item : 5 * item + 5]
        count = len(distances)
        tile = q * chunk_rows + (me ^ distances[0]) // count * (count * width)
        rows = pl.ds(pl.multiple_of(tile, 16), count * width)

        def ship(i, filled):
            copies.append(pltpu.make_async_copy(filled, outs[i].at[rows, :], sems.at[item, i]))
            copies[-1].start()

        def gather(f):
            for d, piece in zip(distances, pieces[item]):
                for c in range(0, width, SUBLANES):
                    top = (me ^ d) % count * width + c
                    to = pl.ds(pl.multiple_of(top, SUBLANES), SUBLANES)
                    for a in range(per):
                        fields[f, to, a * LANES : (a + 1) * LANES] = piece[
                            pl.ds(f * field_rows + c * per + a, SUBLANES, stride=per), :
                        ]

        gather(2)
        ship(4, fields.at[2])
        gather(0)
        conved = fields[0]
        output[...] = (post[rows, :].astype(F32) * conved).astype(BF16)
        ship(0, output)
        d_post[...] = (cotangent[rows, :].astype(F32) * conved).astype(BF16)
        ship(1, d_post)
        gather(1)
        d_gated = fields[1]
        d_pre[...] = (signal[rows, :].astype(F32) * d_gated).astype(BF16)
        ship(2, d_pre)
        d_signal[...] = (pre[rows, :].astype(F32) * d_gated).astype(BF16)
        ship(3, d_signal)
    for copy in copies:
        copy.wait()


def shards(post_gate, pre_gate, signal, cotangent, filter_taps, skip_gain):
    shards_of = lax.axis_size("seq")
    channels, length = post_gate.shape
    chunks = CHUNKS if channels % (CHUNKS * shards_of * SUBLANES) == 0 else 1
    chunk_rows = channels // chunks
    width = chunk_rows // shards_of
    per = length // LANES
    field_rows = width * per
    total_len = shards_of * length
    vmem = pl.BlockSpec(memory_space=pltpu.VMEM)
    hbm = pl.BlockSpec(memory_space=pltpu.HBM)
    params = pltpu.CompilerParams(vmem_limit_bytes=48 * 2**20)

    def swap(pieces):
        moved = {
            d: lax.ppermute(pieces[d], "seq", [(i, i ^ d) for i in range(shards_of)])
            for d in reversed(range(1, shards_of))
        }
        return [pieces[0]] + [moved[d] for d in range(1, shards_of)]

    def rows(count):
        return [jax.ShapeDtypeStruct((count, LANES), F32)] * shards_of

    arrays = (post_gate, pre_gate, signal, cotangent, filter_taps, skip_gain.reshape(1, channels))
    arrived = []
    for q in range(chunks):
        last = q == chunks - 1
        scratch = [pltpu.VMEM((3, chunk_rows, length), F32)]
        if q == 0:
            scratch += [pltpu.VMEM((chunk_rows, length), BF16)] * 4
            scratch += [pltpu.VMEM((chunk_rows, length), F32), pltpu.VMEM((1, channels), F32)]
            scratch += [pltpu.SemaphoreType.DMA((6,))]
        packed = pl.pallas_call(
            functools.partial(pack_kernel, shards_of, chunks, q),
            out_shape=rows(3 * field_rows + SUBLANES * last),
            in_specs=[hbm if q == 0 else vmem] * 6,
            out_specs=[vmem] * shards_of,
            scratch_shapes=scratch,
            compiler_params=params,
        )(*(pltpu.with_memory_space_constraint(x, pltpu.HBM) if q == 0 else x for x in arrays))
        arrived.append(swap(packed))
    consts = [jnp.asarray(t) for t in tables(shards_of, total_len)]
    spectrum_rows = width * shards_of * per
    back = []
    for q in range(chunks):
        last = q == chunks - 1
        mixed = pl.pallas_call(
            functools.partial(spectral_kernel, shards_of, chunks, last, channels, per),
            out_shape=rows(3 * field_rows) + [jax.ShapeDtypeStruct((1, channels), F32)] * last,
            in_specs=[vmem] * (5 + shards_of),
            out_specs=[vmem] * (shards_of + last),
            scratch_shapes=[
                pltpu.VMEM((3 * spectrum_rows, 2 * LANES), F32),
                pltpu.VMEM((3 * spectrum_rows, 4 * LANES), BF16),
            ],
            compiler_params=params,
        )(*consts, *arrived[q])
        if last:
            d_skip = mixed[shards_of]
        back.append(swap(mixed[:shards_of]))
    whole = tuple(range(shards_of))
    if shards_of == 4 and chunks > 1 and width == SUBLANES:
        calls = [[(q, whole) for q in range(chunks - 1)] + [(chunks - 1, (0, 1))]]
        calls.append([(chunks - 1, (2, 3))])
    else:
        calls = [[(q, whole) for q in range(chunks)]]
    outs = []
    for work in calls:
        first = not outs
        taken = [back[q][d] for q, distances in work for d in distances]
        scratch = []
        for _, distances in work:
            count = len(distances) * width
            scratch += [pltpu.VMEM((3, count, length), F32)]
            scratch += [pltpu.VMEM((count, length), BF16)] * 4
        filled = pl.pallas_call(
            functools.partial(gate_kernel, shards_of, chunks, work, first),
            out_shape=[pltpu.HBM((channels, length), BF16)] * 4
            + [pltpu.HBM((channels, length), F32)]
            + [pltpu.HBM((1, channels), F32)] * first,
            in_specs=[vmem] * (5 + len(taken)) + [hbm] * len(outs),
            out_specs=[hbm] * (5 + first),
            scratch_shapes=scratch + [pltpu.SemaphoreType.DMA((len(work), 6))],
            input_output_aliases={5 + len(taken) + i: i for i in range(len(outs))},
            compiler_params=params,
        )(post_gate, pre_gate, signal, cotangent, d_skip, *taken, *outs)
        if first:
            *outs, d_skip_out = filled
        else:
            outs = filled
    output, d_post, d_pre, d_signal, d_filter = outs
    return (output, d_post, d_pre, d_signal, d_skip_out.reshape(channels), d_filter)


def solution(mesh):
    both = P("chan", "seq")
    return jax.shard_map(
        shards,
        mesh=mesh,
        in_specs=(both,) * 5 + (P("chan"),),
        out_specs=(both,) * 4 + (P("chan"), both),
        check_vma=False,
    )
```

```python
import functools
import math

import jax
import jax.numpy as jnp
import ml_dtypes
import numpy as np
from jax import lax
from jax.experimental import pallas as pl
from jax.experimental.pallas import tpu as pltpu
from jax.sharding import PartitionSpec as P

LANES = 128
SUBLANES = 8
CHUNKS = 2
BF16 = jnp.bfloat16
F32 = jnp.float32


def halves(table):
    high = table.astype(np.float32).astype(ml_dtypes.bfloat16)
    low = (table - high.astype(np.float64)).astype(np.float32).astype(ml_dtypes.bfloat16)
    return high, low


def tables(shards_of, total_len):
    blocks = total_len // LANES
    per_shard = blocks // shards_of
    k = np.arange(blocks)[:, None]
    a = np.arange(blocks)[None, :]
    angle = np.pi * (2 * k + 1) * a / (2 * blocks)
    outer = np.concatenate([np.cos(angle), -np.sin(angle)], axis=0)
    inverse = np.concatenate([np.cos(angle).T, -np.sin(angle).T], axis=1) / total_len
    filter_inverse = inverse / math.sqrt(total_len)
    order = [
        np.concatenate(
            [np.arange(per_shard) + (me ^ d) * per_shard for d in range(shards_of)]
        )
        for me in range(shards_of)
    ]

    def wide(table):
        high, low = halves(table)
        return np.concatenate([high, high, low], axis=1)

    outer_w = np.stack([wide(outer[:, o]) for o in order])
    inverse_w = np.stack([wide(inverse[o]) for o in order])
    filter_w = np.stack([wide(filter_inverse[o]) for o in order])
    b = np.arange(LANES)[None, :]
    turn = np.pi * (2 * k + 1) * b / (2 * total_len)
    twiddle = np.stack([np.cos(turn), np.sin(turn)]).astype(np.float32)
    q = np.arange(LANES)
    inner = 2 * np.pi * (q[:, None] * q[None, :] % LANES) / LANES
    dft = np.block([[np.cos(inner), -np.sin(inner)], [np.sin(inner), np.cos(inner)]])
    dft_high, dft_low = halves(dft)
    return outer_w, inverse_w, filter_w, twiddle, np.concatenate([dft_high, dft_low], axis=1)


def triple(x, axis):
    high = x.astype(BF16)
    low = (x - high.astype(F32)).astype(BF16)
    return jnp.concatenate([high, low, high] if axis == 0 else [high, low], axis=axis)


def matmul(a, b):
    return jnp.dot(a, b, preferred_element_type=F32)


def pack_kernel(shards_of, chunks, q, *refs):
    sources, refs = refs[:6], refs[6:]
    outs, (fields, *held) = refs[:shards_of], refs[shards_of:]
    channels, length = sources[0].shape
    chunk_rows = channels // chunks
    last = q == chunks - 1
    if q == 0:
        *held, sems = held
        rows = slice(0, chunk_rows)
        copies = [
            pltpu.make_async_copy(source.at[rows, :] if i < 5 else source, copied, sems.at[i])
            for i, (source, copied) in enumerate(zip(sources, held))
        ]
        for i, copy in enumerate(copies):
            copy.start(priority=i % 2)
        for copy in copies[:4]:
            copy.wait()
        sources = held
    post, pre, signal, cotangent, taps, skip_gain = sources
    me = lax.axis_index("seq")
    width = chunk_rows // shards_of
    per = length // LANES
    field_rows = width * per
    parts = []
    for c in range(0 if last else q * chunk_rows, (q + 1) * chunk_rows, 16):
        rows = slice(c, c + 16)
        g = pre[rows, :].astype(F32) * signal[rows, :].astype(F32)
        dc = cotangent[rows, :].astype(F32) * post[rows, :].astype(F32)
        if c >= q * chunk_rows:
            to = slice(c - q * chunk_rows, c - q * chunk_rows + 16)
            fields[1, to, :] = g
            fields[2, to, :] = dc
        if last:
            prod = g * dc
            parts.append(sum(prod[:, a * LANES : (a + 1) * LANES] for a in range(per)))
    if q == 0:
        for copy in copies[4:]:
            copy.wait()
    turn = lax.broadcasted_iota(jnp.int32, (channels, channels), 0)
    lane = lax.broadcasted_iota(jnp.int32, (channels, channels), 1)
    gains = jnp.broadcast_to(skip_gain[...], (channels, channels))
    gain = jnp.sum(jnp.where(turn == lane, gains, 0.0), axis=1, keepdims=True)
    first = (lax.broadcasted_iota(jnp.int32, (16, LANES), 1) == 0) & (me == 0)
    for c in range(q * chunk_rows, (q + 1) * chunk_rows, 16):
        rows = slice(c, c + 16)
        to = slice(c - q * chunk_rows, c - q * chunk_rows + 16)
        fields[0, to, :] = taps[rows, :]
        fields[0, to, :LANES] = taps[rows, :LANES] + jnp.where(first, gain[rows], 0.0)
    for d in range(shards_of):
        for f in range(3):
            for c in range(0, width, SUBLANES):
                rows = pl.ds(pl.multiple_of((me ^ d) * width + c, SUBLANES), SUBLANES)
                for a in range(per):
                    outs[d][pl.ds(f * field_rows + c * per + a, SUBLANES, stride=per), :] = fields[
                        f, rows, a * LANES : (a + 1) * LANES
                    ]
    if last:
        folded = jnp.concatenate(parts + [jnp.zeros((LANES - channels, LANES), F32)], axis=0)
        skip = jnp.sum(folded.T, axis=0, keepdims=True)
        for d in range(shards_of):
            outs[d][3 * field_rows :, :] = jnp.broadcast_to(skip, (SUBLANES, LANES))


def spectral_kernel(shards_of, chunks, last, channels, per, *refs):
    outer_w, inverse_w, filter_w, twiddle, dft = refs[:5]
    pieces = refs[5 : 5 + shards_of]
    outs = refs[5 + shards_of : 5 + 2 * shards_of]
    rest = refs[5 + 2 * shards_of :]
    if last:
        d_skip, *rest = rest
    spectra, packed = rest
    me = lax.axis_index("seq")
    chunk_rows = channels // chunks
    width = chunk_rows // shards_of
    blocks = shards_of * per
    field_rows = width * per
    spectrum_rows = width * blocks
    cos_t = twiddle[0]
    sin_t = twiddle[1]
    forward = outer_w[me]
    back = (inverse_w[me], inverse_w[me], filter_w[me])
    if last:
        skips = sum(pieces[d][3 * field_rows : 3 * field_rows + 1, :] for d in range(shards_of))
        d_skip[...] = skips[:, : d_skip.shape[1]] * (1.0 / math.sqrt(blocks * LANES))

    def held(f, ch):
        start = f * field_rows + ch * per
        return jnp.concatenate([pieces[d][start : start + per, :] for d in range(shards_of)], axis=0)

    def spectrum(f, ch):
        start = f * spectrum_rows + ch * blocks
        return slice(start, start + blocks)

    def inner(f):
        rows = slice(f * spectrum_rows, (f + 1) * spectrum_rows)
        x = packed[rows, :]
        wide = matmul(x[:, : 2 * LANES], dft[...])
        spectra[rows, :] = (
            wide[:, : 2 * LANES]
            + wide[:, 2 * LANES :]
            + matmul(x[:, 2 * LANES :], dft[:, : 2 * LANES])
        )

    for f in range(3):
        for c in range(0, width, 2):
            x = jnp.concatenate([held(f, c), held(f, c + 1)], axis=1)
            mixed = matmul(forward, triple(x, 0))
            for i in range(2):
                real = mixed[:blocks, i * LANES : (i + 1) * LANES]
                imag = mixed[blocks:, i * LANES : (i + 1) * LANES]
                turned = [real * cos_t + imag * sin_t, imag * cos_t - real * sin_t]
                packed[spectrum(f, c + i), :] = triple(jnp.concatenate(turned, axis=1), 1)
    for f in range(3):
        inner(f)
    for ch in range(width):
        tr, ti = spectra[spectrum(0, ch), :LANES], spectra[spectrum(0, ch), LANES:]
        gr, gi = spectra[spectrum(1, ch), :LANES], spectra[spectrum(1, ch), LANES:]
        dr, di = spectra[spectrum(2, ch), :LANES], spectra[spectrum(2, ch), LANES:]
        products = (
            (gr * tr - gi * ti, gr * ti + gi * tr),
            (tr * dr + ti * di, tr * di - ti * dr),
            (gr * dr + gi * di, gr * di - gi * dr),
        )
        for f, (real, imag) in enumerate(products):
            packed[spectrum(f, ch), :] = triple(jnp.concatenate([imag, real], axis=1), 1)
    for f in range(3):
        inner(f)
    for f in range(3):
        for c in range(0, width, 2):
            turned = []
            for ch in (c, c + 1):
                imag, real = spectra[spectrum(f, ch), :LANES], spectra[spectrum(f, ch), LANES:]
                both = [real * cos_t - imag * sin_t, imag * cos_t + real * sin_t]
                turned.append(jnp.concatenate(both, axis=0))
            y = matmul(back[f], triple(jnp.concatenate(turned, axis=1), 0))
            for i in range(2):
                start = f * field_rows + (c + i) * per
                for d in range(shards_of):
                    outs[d][start : start + per, :] = y[
                        d * per : (d + 1) * per, i * LANES : (i + 1) * LANES
                    ]


def gate_kernel(shards_of, chunks, work, first, *refs):
    post, pre, signal, cotangent, skip = refs[:5]
    refs = refs[5:]
    pieces = []
    for _, distances in work:
        pieces.append(refs[: len(distances)])
        refs = refs[len(distances) :]
    refs = refs[0 if first else 5 :]
    outs, refs = refs[: 5 + first], refs[5 + first :]
    *held, sems = refs
    me = lax.axis_index("seq")
    channels, length = post.shape
    chunk_rows = channels // chunks
    width = chunk_rows // shards_of
    per = length // LANES
    field_rows = width * per
    copies = []
    if first:
        copies.append(pltpu.make_async_copy(skip, outs[5], sems.at[0, 5]))
        copies[0].start()
    for item, (q, distances) in enumerate(work):
        fields, output, d_post, d_pre, d_signal = held[5 * item : 5 * item + 5]
        count = len(distances)
        tile = q * chunk_rows + (me ^ distances[0]) // count * (count * width)
        rows = pl.ds(pl.multiple_of(tile, 16), count * width)

        def ship(i, filled):
            copies.append(pltpu.make_async_copy(filled, outs[i].at[rows, :], sems.at[item, i]))
            copies[-1].start()

        def gather(f):
            for d, piece in zip(distances, pieces[item]):
                for c in range(0, width, SUBLANES):
                    top = (me ^ d) % count * width + c
                    to = pl.ds(pl.multiple_of(top, SUBLANES), SUBLANES)
                    for a in range(per):
                        fields[f, to, a * LANES : (a + 1) * LANES] = piece[
                            pl.ds(f * field_rows + c * per + a, SUBLANES, stride=per), :
                        ]

        gather(2)
        ship(4, fields.at[2])
        gather(0)
        conved = fields[0]
        output[...] = (post[rows, :].astype(F32) * conved).astype(BF16)
        ship(0, output)
        d_post[...] = (cotangent[rows, :].astype(F32) * conved).astype(BF16)
        ship(1, d_post)
        gather(1)
        d_gated = fields[1]
        d_pre[...] = (signal[rows, :].astype(F32) * d_gated).astype(BF16)
        ship(2, d_pre)
        d_signal[...] = (pre[rows, :].astype(F32) * d_gated).astype(BF16)
        ship(3, d_signal)
    for copy in copies:
        copy.wait()


def shards(post_gate, pre_gate, signal, cotangent, filter_taps, skip_gain):
    shards_of = lax.axis_size("seq")
    channels, length = post_gate.shape
    chunks = CHUNKS if channels % (CHUNKS * shards_of * SUBLANES) == 0 else 1
    chunk_rows = channels // chunks
    width = chunk_rows // shards_of
    per = length // LANES
    field_rows = width * per
    total_len = shards_of * length
    vmem = pl.BlockSpec(memory_space=pltpu.VMEM)
    hbm = pl.BlockSpec(memory_space=pltpu.HBM)
    params = pltpu.CompilerParams(vmem_limit_bytes=48 * 2**20)

    def swap(pieces):
        moved = {
            d: lax.ppermute(pieces[d], "seq", [(i, i ^ d) for i in range(shards_of)])
            for d in reversed(range(1, shards_of))
        }
        return [pieces[0]] + [moved[d] for d in range(1, shards_of)]

    def rows(count):
        return [jax.ShapeDtypeStruct((count, LANES), F32)] * shards_of

    arrays = (post_gate, pre_gate, signal, cotangent, filter_taps, skip_gain.reshape(1, channels))
    arrived = []
    for q in range(chunks):
        last = q == chunks - 1
        scratch = [pltpu.VMEM((3, chunk_rows, length), F32)]
        if q == 0:
            scratch += [pltpu.VMEM((chunk_rows, length), BF16)] * 4
            scratch += [pltpu.VMEM((chunk_rows, length), F32), pltpu.VMEM((1, channels), F32)]
            scratch += [pltpu.SemaphoreType.DMA((6,))]
        packed = pl.pallas_call(
            functools.partial(pack_kernel, shards_of, chunks, q),
            out_shape=rows(3 * field_rows + SUBLANES * last),
            in_specs=[hbm if q == 0 else vmem] * 6,
            out_specs=[vmem] * shards_of,
            scratch_shapes=scratch,
            compiler_params=params,
        )(*(pltpu.with_memory_space_constraint(x, pltpu.HBM) if q == 0 else x for x in arrays))
        arrived.append(swap(packed))
    consts = [jnp.asarray(t) for t in tables(shards_of, total_len)]
    spectrum_rows = width * shards_of * per
    back = []
    for q in range(chunks):
        last = q == chunks - 1
        mixed = pl.pallas_call(
            functools.partial(spectral_kernel, shards_of, chunks, last, channels, per),
            out_shape=rows(3 * field_rows) + [jax.ShapeDtypeStruct((1, channels), F32)] * last,
            in_specs=[vmem] * (5 + shards_of),
            out_specs=[vmem] * (shards_of + last),
            scratch_shapes=[
                pltpu.VMEM((3 * spectrum_rows, 2 * LANES), F32),
                pltpu.VMEM((3 * spectrum_rows, 4 * LANES), BF16),
            ],
            compiler_params=params,
        )(*consts, *arrived[q])
        if last:
            d_skip = mixed[shards_of]
        back.append(swap(mixed[:shards_of]))
    whole = tuple(range(shards_of))
    if shards_of == 4 and chunks > 1 and width == SUBLANES:
        calls = [[(q, whole) for q in range(chunks - 1)] + [(chunks - 1, (0, 1))]]
        calls.append([(chunks - 1, (2, 3))])
    else:
        calls = [[(q, whole) for q in range(chunks)]]
    outs = []
    for work in calls:
        first = not outs
        taken = [back[q][d] for q, distances in work for d in distances]
        scratch = []
        for _, distances in work:
            count = len(distances) * width
            scratch += [pltpu.VMEM((3, count, length), F32)]
            scratch += [pltpu.VMEM((count, length), BF16)] * 4
        filled = pl.pallas_call(
            functools.partial(gate_kernel, shards_of, chunks, work, first),
            out_shape=[pltpu.HBM((channels, length), BF16)] * 4
            + [pltpu.HBM((channels, length), F32)]
            + [pltpu.HBM((1, channels), F32)] * first,
            in_specs=[vmem] * (5 + len(taken)) + [hbm] * len(outs),
            out_specs=[hbm] * (5 + first),
            scratch_shapes=scratch + [pltpu.SemaphoreType.DMA((len(work), 6))],
            input_output_aliases={5 + len(taken) + i: i for i in range(len(outs))},
            compiler_params=params,
        )(post_gate, pre_gate, signal, cotangent, d_skip, *taken, *outs)
        if first:
            *outs, d_skip_out = filled
        else:
            outs = filled
    output, d_post, d_pre, d_signal, d_filter = outs
    return (output, d_post, d_pre, d_signal, d_skip_out.reshape(channels), d_filter)


def solution(mesh):
    both = P("chan", "seq")
    return jax.shard_map(
        shards,
        mesh=mesh,
        in_specs=(both,) * 5 + (P("chan"),),
        out_specs=(both,) * 4 + (P("chan"), both),
        check_vma=False,
    )
```
